256 devices in a mesh: ctx: 128 (over x, y, z), head: 2 (over core).
Axes of the slice: x: 4, y: 4, z: 8, core: 2. Of those that a mesh axis runs over, the one named last changes fastest.
Arguments:
- tokens: float32 [32768, 512], P('ctx', 'head'), may hold values from -21 to 21
- w_query: float32 [512, 512], P(None, 'head'), may hold values from -2 to 2
- w_key: float32 [512, 512], P(None, 'head'), may hold values from -2 to 2
- w_value: float32 [512, 512], P(None, 'head'), may hold values from -0.25 to 0.25
- w_out: float32 [512, 512], P('head'), may hold values from -0.25 to 0.25
- grad_out: float32 [32768, 512], P('ctx', 'head'), may hold values from -6 to 6
Outputs:
- layer_out: float32 [32768, 512], P('ctx', 'head')
- grad_tokens: float32 [32768, 512], P('ctx', 'head')
- grad_query: float32 [512, 512], P(None, 'head')
- grad_key: float32 [512, 512], P(None, 'head')
- grad_value: float32 [512, 512], P(None, 'head')
- grad_out_weight: float32 [512, 512], P('head')
The draws below stay inside these ranges and needn't reach their ends.
All inputs are finite; a program needn't handle non-finite values.
Results may differ from the reference program's by a relative error of at most 0.0003.
Values sent between devices are 32-bit elements; how exact they have to be, the bound alone decides.
No kernel may reach another device: no remote copies, remote signals or barrier semaphores. Data moves between devices by JAX's collectives and lax.ppermute only.
A program may use at most 64 MiB of HBM per device.

```python
import math
import jax
import jax.numpy as jnp
from jax import lax

HEADS = 8
HEAD_DIM = 64
D = 512
BLOCK = 128
LEVELS = 3
TOKENS = 32768


def shared_base(key):
    return jnp.clip(jax.random.normal(key, (D, D), jnp.float32), -4.0, 4.0)


def draw_w_query(key, part):
    base_matrix = shared_base(key)
    return 2.0 * base_matrix / math.sqrt(D)


def draw_w_key(key, part):
    key = jax.random.fold_in(key, 7)
    other_matrix = jnp.clip(jax.random.normal(key, (D, D), jnp.float32), -4.0, 4.0)
    return 2.0 * other_matrix / math.sqrt(D)


def draw_tokens(key, part):
    key = jax.random.fold_in(key, 3)
    first_key = jax.random.fold_in(key, 0)
    normal_rows = jnp.clip(jax.random.normal(first_key, (TOKENS, D), jnp.float32), -5.0, 5.0)
    return normal_rows


def level_of(stream_key, extent, cuts, smallest, top_value):
    loudness = 1.0
    for position, parts in cuts:
        steps = jax.random.uniform(jax.random.fold_in(jax.random.fold_in(stream_key, 6), position), (parts,), jnp.float32, smallest / len(cuts), top_value / len(cuts))
        loudness = loudness * jnp.repeat(jnp.exp(steps), extent[position] // parts).reshape((-1,) + (1,) * (len(extent) - 1 - position))
    return loudness


def centred(rng, extent, scale, most, cuts=(), kind=jnp.bfloat16):
    array = scale * jax.random.normal(rng, extent, jnp.float32)
    if cuts:
        array = array * level_of(rng, extent, cuts, -0.22, 0.18)
    return jnp.clip(array, -most, most).astype(kind)


def setup_inputs(seed: int = 0) -> dict:
    key_list = jax.random.split(jax.random.key(seed), 7)
    return {
        "tokens": draw_tokens(jax.random.fold_in(key_list[6], 71), 0),
        "w_query": draw_w_query(jax.random.fold_in(key_list[6], 71), 0),
        "w_key": draw_w_key(jax.random.fold_in(key_list[6], 71), 0),
        "w_value": centred(key_list[3], (D, D), D ** -0.5, 0.25, ((1, 2),), jnp.float32),
        "w_out": centred(key_list[4], (D, D), D ** -0.5, 0.25, ((0, 2),), jnp.float32),
        "grad_out": centred(key_list[5], (TOKENS, D), 1.0, 6.0, ((0, 128), (1, 2)), jnp.float32),
    }


masked_score = -1e+30

def halve(values):
    paired = values.reshape(values.shape[0] // 2, 2, values.shape[1])
    return 0.5 * (paired[:, 0] + paired[:, 1])

def block_attend(queries, key_block, value_block, alive_mask, head_count):
    block_count, query_count, feat_width = queries.shape
    key_count = key_block.shape[1]
    head_width = feat_width // head_count
    query_heads = queries.reshape(block_count, query_count, head_count, head_width)
    key_heads = key_block.reshape(block_count, key_count, head_count, head_width)
    value_heads = value_block.reshape(block_count, key_count, head_count, head_width)
    scores = jnp.einsum('brhe,bmhe->bhrm', query_heads, key_heads, precision=lax.Precision.HIGHEST) * head_width ** (-0.5)
    key_mask = alive_mask[:, None, None, :] > 0.5
    scores = jnp.where(key_mask, scores, masked_score)
    row_peak = lax.stop_gradient(lax.optimization_barrier(jnp.max(scores, axis=-1)))
    weights = jnp.where(key_mask, jnp.exp(scores - row_peak[..., None]), 0.0)
    numerator = jnp.einsum('bhrm,bmhe->brhe', weights, value_heads, precision=lax.Precision.HIGHEST)
    denominator = lax.optimization_barrier(jnp.sum(weights, axis=-1))
    return (numerator, jnp.swapaxes(denominator, 1, 2), jnp.swapaxes(row_peak, 1, 2))

def combine(pieces):
    peaks = []
    for degree, piece in enumerate(pieces):
        peaks.append(jnp.repeat(piece[2], 2 ** degree, axis=0))
    overall_peak = peaks[0]
    for later_peak in peaks[1:]:
        overall_peak = jnp.maximum(overall_peak, later_peak)
    overall_peak = lax.stop_gradient(overall_peak)
    numerator = 0.0
    denominator = 0.0
    for degree, piece in enumerate(pieces):
        factor = 2.0 ** degree * jnp.exp(peaks[degree] - overall_peak)
        numerator = numerator + factor[..., None] * jnp.repeat(piece[0], 2 ** degree, axis=0)
        denominator = denominator + factor * jnp.repeat(piece[1], 2 ** degree, axis=0)
    attended = numerator / denominator[..., None]
    return attended.reshape(attended.shape[0], -1)

def level_terms(queries, key_rows, value_rows, degree):
    count_rows, feat_width = queries.shape
    block_count = count_rows // BLOCK
    zero_rim = jnp.zeros((BLOCK, feat_width), jnp.float32)
    key_padded = jnp.concatenate([zero_rim, key_rows, zero_rim])
    value_padded = jnp.concatenate([zero_rim, value_rows, zero_rim])
    unit_mask = jnp.ones((BLOCK,), jnp.float32)

    def one_block(block_index):
        row_start = block_index * BLOCK
        block_queries = lax.dynamic_slice_in_dim(queries, row_start, BLOCK, 0)
        near_keys = lax.dynamic_slice_in_dim(key_padded, row_start, 3 * BLOCK, 0)
        near_values = lax.dynamic_slice_in_dim(value_padded, row_start, 3 * BLOCK, 0)
        left_alive = (block_index > 0).astype(jnp.float32) * unit_mask
        right_alive = (block_index < block_count - 1).astype(jnp.float32) * unit_mask
        if degree == 0:
            alive_mask = jnp.concatenate([left_alive, unit_mask, right_alive])
        else:
            near_keys = jnp.concatenate([near_keys[:BLOCK], near_keys[2 * BLOCK:]])
            near_values = jnp.concatenate([near_values[:BLOCK], near_values[2 * BLOCK:]])
            alive_mask = jnp.concatenate([left_alive, right_alive])
        return block_attend(block_queries[None], near_keys[None], near_values[None], alive_mask[None], HEADS)
    numerator, denominator, row_peak = lax.map(jax.checkpoint(one_block), jnp.arange(block_count, dtype=jnp.int32))
    return (numerator.reshape(count_rows, HEADS, HEAD_DIM), denominator.reshape(count_rows, HEADS), row_peak.reshape(count_rows, HEADS))

def forward(tokens, w_query, w_key, w_value, w_out):
    query_rows = jnp.dot(tokens, w_query, preferred_element_type=jnp.float32, precision=lax.Precision.HIGHEST)
    key_rows = jnp.dot(tokens, w_key, preferred_element_type=jnp.float32, precision=lax.Precision.HIGHEST)
    value_rows = jnp.dot(tokens, w_value, preferred_element_type=jnp.float32, precision=lax.Precision.HIGHEST)
    pieces = []
    for degree in range(LEVELS + 1):
        if degree > 0:
            query_rows = halve(query_rows)
            key_rows = halve(key_rows)
            value_rows = halve(value_rows)
        pieces.append(level_terms(query_rows, key_rows, value_rows, degree))
    attended = combine(pieces)
    return jnp.dot(attended, w_out, preferred_element_type=jnp.float32, precision=lax.Precision.HIGHEST)

def reference(tokens, w_query, w_key, w_value, w_out, grad_out):
    layer_out, pull_back = jax.vjp(forward, tokens, w_query, w_key, w_value, w_out)
    grad_tokens, grad_query, grad_key, grad_value, grad_out_weight = pull_back(grad_out)
    factor = TOKENS ** (-0.5)
    return (layer_out, grad_tokens, grad_query * factor, grad_key * factor, grad_value * factor, grad_out_weight * factor)
```

```python
import functools
import jax
import jax.numpy as jnp
from jax import lax
from jax.experimental import pallas as pl
from jax.experimental.pallas import tpu as pltpu
from jax.sharding import PartitionSpec as P

HEAD_DIM = 64
BLOCK = 128
LEVELS = 3
F32 = jnp.float32
BF16 = jnp.bfloat16
MASKED = -1e30

NN = ((1,), (0,))
NT = ((1,), (1,))
TN = ((0,), (0,))


def split(value):
    high = value.astype(BF16)
    return high, (value - high.astype(F32)).astype(BF16)


def mm(a, b, dims):
    def dot(u, v):
        return lax.dot_general(u, v, (dims, ((), ())), preferred_element_type=F32)

    return dot(a[0], b[0]) + (dot(a[0], b[1]) + dot(a[1], b[0]))


def cut(pair, rows):
    return pair[0][rows], pair[1][rows]


def head_masks(rows, width, heads, dtype=F32):
    lane = lax.broadcasted_iota(jnp.int32, (rows, width), 1) // HEAD_DIM
    return [lane == h for h in range(heads)]


def stack_heads(value, heads):
    masks = head_masks(value.shape[0], value.shape[1], heads)
    return jnp.concatenate([jnp.where(m, value, 0.0) for m in masks], axis=0)


def unstack(value, heads, width):
    rows = value.shape[0] // heads
    masks = head_masks(rows, width, heads)
    out = jnp.zeros((rows, width), F32)
    for h, m in enumerate(masks):
        out = jnp.where(m, value[h * rows : (h + 1) * rows], out)
    return out


def stack_column(value, heads):
    lane = lax.broadcasted_iota(jnp.int32, value.shape, 1)
    return jnp.concatenate(
        [
            jnp.sum(jnp.where(lane == h * HEAD_DIM, value, 0.0), axis=1, keepdims=True)
            for h in range(heads)
        ],
        axis=0,
    )


def expand(buf, value, times):
    if times == 1:
        return value
    rows = value.shape[0]
    for half in range(value.shape[1] // 128):
        for j in range(times):
            buf[half, pl.ds(j, rows, stride=times), :] = value[:, half * 128 : half * 128 + 128]
    return jnp.concatenate(
        [buf[half, : rows * times, :] for half in range(value.shape[1] // 128)], axis=1
    )


def pool(buf, value, times):
    if times == 1:
        return value
    rows = value.shape[0] // times
    parts = []
    for half in range(value.shape[1] // 128):
        buf[half, : value.shape[0], :] = value[:, half * 128 : half * 128 + 128]
        total = buf[half, pl.ds(0, rows, stride=times), :]
        for j in range(1, times):
            total = total + buf[half, pl.ds(j, rows, stride=times), :]
        parts.append(total)
    return jnp.concatenate(parts, axis=1)


def attend_kernel(
    place_ref, x_ref, wq_ref, wk_ref, wv_ref, wo_ref,
    mine_ref, theirs_ref, dw_ref,
    q_s, k_s, v_s, dk_s, dv_s, xh_s, xl_s, wh_s, wl_s, buf, *, count, scale,
):
    own, width = q_s.shape
    total = k_s.shape[0]
    near = 3 * own
    heads = width // HEAD_DIM
    place = place_ref[0]
    core = place_ref[1]
    line = lax.rem(place, 8)
    turn = jnp.where(line >= 4, own, 0)
    pair = BLOCK * lax.div(lax.rem(line, 4), 2)

    def window(row):
        return pl.multiple_of(near + lax.rem(row + turn, near), BLOCK)

    level_2 = [window(BLOCK + pair), window(3 * BLOCK + pair)]
    level_3 = [window(0), window(2 * own)]

    for c in range(2):
        for start in range(0, near, own):
            h, l = split(x_ref[c, start : start + own])
            xh_s[c, start : start + own] = h
            xl_s[c, start : start + own] = l
        for j in range(2):
            at = slice(near + j * BLOCK, near + (j + 1) * BLOCK)
            xh_s[c, at], xl_s[c, at] = split(x_ref[c, pl.ds(level_2[j], BLOCK)])
            at = slice(near + (j + 2) * BLOCK, near + (j + 3) * BLOCK)
            xh_s[c, at], xl_s[c, at] = split(
                0.5 * pool(buf, x_ref[c, pl.ds(level_3[j], 2 * BLOCK)], 2)
            )
        for k, w_ref in enumerate((wq_ref, wk_ref, wv_ref)):
            wh_s[k, c], wl_s[k, c] = split(w_ref[c * width : (c + 1) * width])
        wh_s[3, c], wl_s[3, c] = split(wo_ref[:, c * width : (c + 1) * width])

    def weight(k, c):
        return wh_s[k, c], wl_s[k, c]

    def rows_of(c, start, size):
        return xh_s[c, start : start + size], xl_s[c, start : start + size]

    def project(k, start):
        return mm(rows_of(0, start, own), weight(k, 0), NN) + mm(
            rows_of(1, start, own), weight(k, 1), NN
        )

    q_s[...] = project(0, own) * HEAD_DIM ** (-0.5)
    for start in range(0, total, own):
        k_s[start : start + own] = project(1, start)
        v_s[start : start + own] = project(2, start)

    jobs = []
    for b in range(own // BLOCK):
        jobs.append((0, b))
    for level in range(1, LEVELS + 1):
        jobs.append((level, 0))
    queries = [q_s[...]]
    for level in range(1, LEVELS + 1):
        queries.append(pool(buf, q_s[...], 2**level) * 2.0**-level)

    def keys_of(level, b, ref):
        if level == 0:
            start = own - BLOCK + b * BLOCK
            return ref[start : start + 3 * BLOCK]
        if level == 1:
            return jnp.concatenate(
                [0.5 * pool(buf, ref[:own], 2), 0.5 * pool(buf, ref[2 * own : 3 * own], 2)]
            )
        start = 3 * own + (level - 2) * 2 * BLOCK
        return ref[start : start + 2 * BLOCK]

    def bias_of(level, b):
        span = 1 if level <= 1 else 2 ** (level - 1)
        left_dead = place < span
        right_dead = place >= count - span
        keys = 3 * BLOCK if level == 0 else 2 * BLOCK
        if level == 0 and b > 0:
            left_dead = False
        if level == 0 and b < own // BLOCK - 1:
            right_dead = False
        col = lax.broadcasted_iota(jnp.int32, (1, keys), 1)
        bias = jnp.zeros((1, keys), F32)
        if left_dead is not False:
            bias = jnp.where(jnp.logical_and(col < BLOCK, left_dead), MASKED, bias)
        if right_dead is not False:
            bias = jnp.where(jnp.logical_and(col >= keys - BLOCK, right_dead), MASKED, bias)
        return bias

    saved = []
    peaks, dens, nums = [], [], []
    for level, b in jobs:
        rows = BLOCK if level == 0 else queries[level].shape[0]
        query = split(stack_heads(queries[level][b * rows : (b + 1) * rows], heads))
        key = split(keys_of(level, b, k_s))
        value = split(keys_of(level, b, v_s))
        scores = mm(query, key, NT) + bias_of(level, b)
        peak = jnp.max(scores, axis=1, keepdims=True)
        weights = jnp.exp(scores - peak)
        den = jnp.sum(weights, axis=1, keepdims=True)
        halves = split(weights)
        num = unstack(mm(halves, value, NN), heads, width)
        saved.append((query, key, value, weights, halves))
        peaks.append(unstack(peak, heads, width))
        dens.append(unstack(den, heads, width))
        nums.append(num)
    blocks = own // BLOCK
    join = lambda parts: [jnp.concatenate(parts[:blocks])] + parts[blocks:]
    peaks, dens, nums = join(peaks), join(dens), join(nums)
    wide_peaks = [expand(buf, p, 2**l) for l, p in enumerate(peaks)]
    top = functools.reduce(jnp.maximum, wide_peaks)
    factors = [2.0**l * jnp.exp(p - top) for l, p in enumerate(wide_peaks)]
    num = sum(f * expand(buf, n, 2**l) for l, (f, n) in enumerate(zip(factors, nums)))
    den = sum(f * expand(buf, n, 2**l) for l, (f, n) in enumerate(zip(factors, dens)))
    inverse = 1.0 / den
    attended = num * inverse
    att = split(attended)

    go = [split(x_ref[c, 2 * near : 2 * near + own]) for c in range(2)]
    d_att = jnp.zeros((own, width), F32)
    for c in range(2):
        d_att = d_att + mm(go[c], weight(3, c), NT)
        dw_ref[3, c] = mm(att, go[c], TN) * scale
    for target, c in ((theirs_ref, 1 - core), (mine_ref, core)):
        target[2 * near : 2 * near + own] = mm(att, weight(3, c), NN)

    r = lax.broadcasted_iota(jnp.int32, (width, width), 0) // HEAD_DIM
    s = lax.broadcasted_iota(jnp.int32, (width, width), 1) // HEAD_DIM
    ones = jnp.where(r == s, 1.0, 0.0).astype(BF16)
    prod = d_att * attended
    p0, p1 = split(prod)
    delta = lax.dot_general(p0, ones, (NN, ((), ())), preferred_element_type=F32)
    delta = delta + lax.dot_general(p1, ones, (NN, ((), ())), preferred_element_type=F32)

    dk_s[...] = jnp.zeros_like(dk_s)
    dv_s[...] = jnp.zeros_like(dv_s)
    d_query = jnp.zeros((own, width), F32)
    level_dq = [[] for _ in range(LEVELS + 1)]
    for (level, b), (query, key, value, weights, halves) in zip(jobs, saved):
        if b == 0:
            share = factors[level] * inverse
            d_num = pool(buf, share * d_att, 2**level)
            d_den = pool(buf, -share * delta, 2**level)
        rows = BLOCK if level == 0 else d_num.shape[0]
        part = slice(b * rows, (b + 1) * rows)
        grad = split(stack_heads(d_num[part], heads))
        d_scores = split(weights * (mm(grad, value, NT) + stack_column(d_den[part], heads)))
        d_value = mm(halves, grad, TN)
        d_key = mm(d_scores, query, TN)
        level_dq[level].append(unstack(mm(d_scores, key, NN), heads, width))
        for ref, grads in ((dk_s, d_key), (dv_s, d_value)):
            if level == 0:
                start = own - BLOCK + b * BLOCK
                ref[start : start + 3 * BLOCK] += grads
            elif level == 1:
                ref[:own] += expand(buf, 0.5 * grads[:BLOCK], 2)
                ref[2 * own : 3 * own] += expand(buf, 0.5 * grads[BLOCK:], 2)
            else:
                start = 3 * own + (level - 2) * 2 * BLOCK
                ref[start : start + 2 * BLOCK] += grads
    for level, parts in enumerate(level_dq):
        d_query = d_query + expand(buf, jnp.concatenate(parts) * 2.0**-level, 2**level)
    dq = split(d_query * HEAD_DIM ** (-0.5))
    dk = split(dk_s[...])
    dv = split(dv_s[...])
    for c in range(2):
        dw_ref[0, c] = mm(rows_of(c, own, own), dq, TN) * scale
        dw_ref[1, c] = mm(rows_of(c, 0, total), dk, TN) * scale
        dw_ref[2, c] = mm(rows_of(c, 0, total), dv, TN) * scale
    for target, c in ((theirs_ref, 1 - core), (mine_ref, core)):
        target[near : 2 * near] = jnp.zeros((near, width), F32)
        for start in range(0, total, own):
            rows = slice(start, start + own)
            dx = mm(cut(dk, rows), weight(1, c), NT) + mm(cut(dv, rows), weight(2, c), NT)
            if start == own:
                dx = dx + mm(dq, weight(0, c), NT)
            if start < near:
                target[rows] = dx
                continue
            for j in range(2):
                part = dx[j * BLOCK : (j + 1) * BLOCK]
                if start == near:
                    target[pl.ds(level_2[j], BLOCK)] += part
                else:
                    target[pl.ds(level_3[j], 2 * BLOCK)] += expand(buf, 0.5 * part, 2)


def attend(place, x, wq, wk, wv, wo, count, scale):
    _, rows, half = x.shape
    own = rows // 7
    total = 5 * own
    width = wq.shape[1]
    vmem = pl.BlockSpec(memory_space=pltpu.VMEM)

    def shape(*s):
        return jax.ShapeDtypeStruct(s, F32)

    return pl.pallas_call(
        functools.partial(attend_kernel, count=count, scale=scale),
        out_shape=(shape(rows, half), shape(rows, half), shape(4, 2, half, width)),
        in_specs=[pl.BlockSpec(memory_space=pltpu.SMEM)] + [vmem] * 5,
        out_specs=(vmem,) * 3,
        scratch_shapes=[
            pltpu.VMEM((own, width), F32),
            pltpu.VMEM((total, width), F32),
            pltpu.VMEM((total, width), F32),
            pltpu.VMEM((total, width), F32),
            pltpu.VMEM((total, width), F32),
            pltpu.VMEM((2, total, half), BF16),
            pltpu.VMEM((2, total, half), BF16),
            pltpu.VMEM((4, 2, half, width), BF16),
            pltpu.VMEM((4, 2, half, width), BF16),
            pltpu.VMEM((width // 128, own, 128), F32),
        ],
        compiler_params=pltpu.CompilerParams(vmem_limit_bytes=48 * 2**20),
        cost_estimate=pl.CostEstimate(
            flops=12 * 10**9, bytes_accessed=16 * 2**20, transcendentals=10**6
        ),
    )(place, x, wq, wk, wv, wo)


LINE = ("zh", "zl")
CTX = ("x", "y", "zh", "zl")
WIDE = ("x", "y", "zl")
SWAP = [(0, 1), (1, 0)]


def spread(rows, axes, parts):
    return lax.all_to_all(jnp.broadcast_to(rows[None], (parts,) + rows.shape), axes, 0, 0)


def local(tokens, w_query, w_key, w_value, w_out, grad_out):
    count = lax.axis_size(CTX)
    place = lax.axis_index(CTX)
    core = lax.axis_index("head")
    own, half = tokens.shape
    near = 3 * own
    quarter = own // 4
    low = place % 8 < 4
    ahead = [(i, i + 1) for i in range(count - 1)]
    back = [(j, i) for i, j in ahead]
    across = []
    for i in range(count - 8):
        across.append((i, i + 8) if i % 8 < 4 else (i + 8, i))
    home = [(j, i) for i, j in across]

    from_left = lax.ppermute(tokens, CTX, ahead)
    from_right = lax.ppermute(tokens, CTX, back)
    pooled = 0.25 * tokens.reshape(quarter, 4, half).sum(1)
    line = spread(pooled, LINE, 8).reshape(2, own, half)
    got = lax.ppermute(jnp.where(low, line[1], line[0]), CTX, across)
    x = jnp.concatenate([from_left, tokens, from_right, got, line[0], line[1], grad_out])
    x = lax.all_gather(x, "head")
    where = jnp.stack([place, core]).astype(jnp.int32)
    scale = (own * count) ** (-0.5)
    mine, theirs, dw = attend(where, x, w_query, w_key, w_value, w_out, count, scale)

    both = mine + lax.ppermute(theirs, "head", SWAP)
    layer_out = both[2 * near :]
    to_left = lax.ppermute(both[:own], CTX, back)
    to_right = lax.ppermute(both[2 * own : near], CTX, ahead)
    given = lax.ppermute(both[near : near + own], CTX, home)
    lined = both[near + own : 2 * near].reshape(2, own, half)
    lined = lined + jnp.stack([jnp.where(low, 0.0, given), jnp.where(low, given, 0.0)])
    pooled = lax.psum_scatter(lined.reshape(8, quarter, half), LINE, scatter_dimension=0)
    pooled = jnp.broadcast_to(0.25 * pooled[:, None], (quarter, 4, half)).reshape(own, half)
    grad_tokens = both[own : 2 * own] + to_left + to_right + pooled

    wide = lax.axis_size(WIDE)
    chunk = lax.all_to_all(dw.reshape(wide, -1, half), WIDE, 0, 0).sum(0)
    chunk = spread(chunk, "zh", 4).sum(0)
    dw = spread(chunk, WIDE, wide).reshape(4, 2 * half, half)
    return (
        layer_out,
        grad_tokens,
        dw[0],
        dw[1],
        dw[2],
        jnp.concatenate([dw[3, :half], dw[3, half:]], axis=1),
    )


def solution(mesh):
    lines = mesh.shape["ctx"] // 8
    split_mesh = jax.sharding.Mesh(
        mesh.devices.reshape(-(-lines // 4), min(lines, 4), 4, 2, 2), ("x", "y", "zh", "zl", "head")
    )
    placed = (
        P(CTX, "head"),
        P(None, "head"),
        P(None, "head"),
        P(None, "head"),
        P("head", None),
        P(CTX, "head"),
    )
    return jax.shard_map(
        local,
        mesh=split_mesh,
        in_specs=placed,
        out_specs=(P(CTX, "head"),) * 2 + (P(None, "head"),) * 3 + (P("head", None),),
        check_vma=False,
    )
```

```python
import functools
import jax
import jax.numpy as jnp
from jax import lax
from jax.experimental import pallas as pl
from jax.experimental.pallas import tpu as pltpu
from jax.sharding import PartitionSpec as P

HEAD_DIM = 64
BLOCK = 128
LEVELS = 3
F32 = jnp.float32
BF16 = jnp.bfloat16
MASKED = -1e30

NN = ((1,), (0,))
NT = ((1,), (1,))
TN = ((0,), (0,))


def split(value):
    high = value.astype(BF16)
    return high, (value - high.astype(F32)).astype(BF16)


def mm(a, b, dims):
    def dot(u, v):
        return lax.dot_general(u, v, (dims, ((), ())), preferred_element_type=F32)

    return dot(a[0], b[0]) + (dot(a[0], b[1]) + dot(a[1], b[0]))


def cut(pair, rows):
    return pair[0][rows], pair[1][rows]


def head_masks(rows, width, heads, dtype=F32):
    lane = lax.broadcasted_iota(jnp.int32, (rows, width), 1) // HEAD_DIM
    return [lane == h for h in range(heads)]


def stack_heads(value, heads):
    masks = head_masks(value.shape[0], value.shape[1], heads)
    return jnp.concatenate([jnp.where(m, value, 0.0) for m in masks], axis=0)


def unstack(value, heads, width):
    rows = value.shape[0] // heads
    masks = head_masks(rows, width, heads)
    out = jnp.zeros((rows, width), F32)
    for h, m in enumerate(masks):
        out = jnp.where(m, value[h * rows : (h + 1) * rows], out)
    return out


def stack_column(value, heads):
    lane = lax.broadcasted_iota(jnp.int32, value.shape, 1)
    return jnp.concatenate(
        [
            jnp.sum(jnp.where(lane == h * HEAD_DIM, value, 0.0), axis=1, keepdims=True)
            for h in range(heads)
        ],
        axis=0,
    )


def expand(buf, value, times):
    if times == 1:
        return value
    rows = value.shape[0]
    for half in range(value.shape[1] // 128):
        for j in range(times):
            buf[half, pl.ds(j, rows, stride=times), :] = value[:, half * 128 : half * 128 + 128]
    return jnp.concatenate(
        [buf[half, : rows * times, :] for half in range(value.shape[1] // 128)], axis=1
    )


def pool(buf, value, times):
    if times == 1:
        return value
    rows = value.shape[0] // times
    parts = []
    for half in range(value.shape[1] // 128):
        buf[half, : value.shape[0], :] = value[:, half * 128 : half * 128 + 128]
        total = buf[half, pl.ds(0, rows, stride=times), :]
        for j in range(1, times):
            total = total + buf[half, pl.ds(j, rows, stride=times), :]
        parts.append(total)
    return jnp.concatenate(parts, axis=1)


def kept_left(place, core):
    return lax.rem(place, 2) != core


def near_kernel(place_ref, *refs):
    x_refs = (refs[:3], refs[3:6])
    w_refs = refs[6:10]
    wh_ref, wl_ref, xh_ref, xl_ref, gh_ref, gl_ref, q_ref, k_ref, v_ref, d_ref = refs[10:]
    core = place_ref[1]
    own, width = q_ref.shape
    for c in range(2):
        for k, w_ref in enumerate(w_refs[:3]):
            wh_ref[k, c], wl_ref[k, c] = split(w_ref[c * width : (c + 1) * width])
        wh_ref[3, c], wl_ref[3, c] = split(w_refs[3][:, c * width : (c + 1) * width])
    here = kept_left(place_ref[0], core)
    for side, (own_ref, go_ref, _) in enumerate(x_refs):
        kept, other = x_refs[0][2][side], x_refs[1][2][1 - side]
        left = jnp.where(here, kept, other)
        right = jnp.where(here, other, kept)
        for j, x in enumerate((left, own_ref[...], right)):
            rows = slice(j * own, (j + 1) * own)
            xh_ref[side, rows], xl_ref[side, rows] = split(x)
        gh_ref[side], gl_ref[side] = split(go_ref[...])

    def weight(k, c):
        return wh_ref[k, c], wl_ref[k, c]

    def project(k, start):
        rows = slice(start, start + own)
        return mm((xh_ref[0, rows], xl_ref[0, rows]), weight(k, core), NN) + mm(
            (xh_ref[1, rows], xl_ref[1, rows]), weight(k, 1 - core), NN
        )

    q_ref[...] = project(0, own) * HEAD_DIM ** (-0.5)
    for start in range(0, 3 * own, own):
        k_ref[start : start + own] = project(1, start)
        v_ref[start : start + own] = project(2, start)
    d_ref[...] = mm((gh_ref[0], gl_ref[0]), weight(3, core), NT) + mm(
        (gh_ref[1], gl_ref[1]), weight(3, 1 - core), NT
    )


def near(place, xs, weights):
    own, half = xs[0].shape
    width = weights[0].shape[1]
    vmem = pl.BlockSpec(memory_space=pltpu.VMEM)

    def shape(kind, *s):
        return jax.ShapeDtypeStruct(s, kind)

    return pl.pallas_call(
        near_kernel,
        out_shape=(
            shape(BF16, 4, 2, half, width),
            shape(BF16, 4, 2, half, width),
            shape(BF16, 2, 3 * own, half),
            shape(BF16, 2, 3 * own, half),
            shape(BF16, 2, own, half),
            shape(BF16, 2, own, half),
            shape(F32, own, width),
            shape(F32, 3 * own, width),
            shape(F32, 3 * own, width),
            shape(F32, own, width),
        ),
        in_specs=[pl.BlockSpec(memory_space=pltpu.SMEM)] + [vmem] * 10,
        out_specs=(vmem,) * 10,
        compiler_params=pltpu.CompilerParams(vmem_limit_bytes=24 * 2**20),
        cost_estimate=pl.CostEstimate(
            flops=3 * 10**9, bytes_accessed=10 * 2**20, transcendentals=0
        ),
    )(place, *xs, *weights)


def attend_kernel(
    place_ref, *refs, count, scale,
):
    far_refs = (refs[:2], refs[2:4])
    wh_ref, wl_ref, xh_ref, xl_ref, gh_ref, gl_ref, q_ref, k_ref, v_ref, d_ref = refs[4:14]
    mine_ref, theirs_ref, dw_ref = refs[14:17]
    k_s, v_s, dk_s, dv_s, xh_s, xl_s, buf, win_s = refs[17:]
    own, width = q_ref.shape
    near = 3 * own
    far = 4 * BLOCK
    heads = width // HEAD_DIM
    place = place_ref[0]
    core = place_ref[1]
    line = lax.rem(place, 8)
    sides = ((0, core), (1, 1 - core))
    turn = jnp.where(line >= 4, own, 0)
    pair = BLOCK * lax.div(lax.rem(line, 4), 2)

    def window(row, base=0):
        return pl.multiple_of(base + lax.rem(row + turn, near), BLOCK)

    level_2 = (BLOCK + pair, 3 * BLOCK + pair)
    level_3 = (0, 2 * own)
    for side, (got_ref, line_ref) in enumerate(far_refs):
        win_s[:own] = got_ref[...]
        win_s[own:] = line_ref[...]
        parts = [win_s[pl.ds(window(row), BLOCK)] for row in level_2]
        parts += [0.5 * pool(buf, win_s[pl.ds(window(row), 2 * BLOCK)], 2) for row in level_3]
        for j, part in enumerate(parts):
            rows = slice(j * BLOCK, (j + 1) * BLOCK)
            xh_s[side, rows], xl_s[side, rows] = split(part)

    def weight(k, c):
        return wh_ref[k, c], wl_ref[k, c]

    def far_rows(side, rows=slice(None)):
        return xh_s[side, rows], xl_s[side, rows]

    for start in range(0, far, own):
        rows = slice(start, start + own)
        for k, ref in ((1, k_s), (2, v_s)):
            ref[rows] = sum(mm(far_rows(s, rows), weight(k, c), NN) for s, c in sides)

    jobs = []
    for b in range(own // BLOCK):
        jobs.append((0, b))
    for level in range(1, LEVELS + 1):
        jobs.append((level, 0))
    queries = [q_ref[...]]
    for level in range(1, LEVELS + 1):
        queries.append(pool(buf, q_ref[...], 2**level) * 2.0**-level)

    def keys_of(level, b, ref):
        if level == 0:
            start = own - BLOCK + b * BLOCK
            return ref[0][start : start + 3 * BLOCK]
        if level == 1:
            return jnp.concatenate(
                [0.5 * pool(buf, ref[0][:own], 2), 0.5 * pool(buf, ref[0][2 * own :], 2)]
            )
        start = (level - 2) * 2 * BLOCK
        return ref[1][start : start + 2 * BLOCK]

    def bias_of(level, b):
        keys = 3 * BLOCK if level == 0 else 2 * BLOCK
        col = lax.broadcasted_iota(jnp.int32, (1, keys), 1)
        left, right = place < 1, place >= count - 1
        if level > 1:
            span = 2 ** (level - 1)
            left, right = place < span, place >= count - span
        if level == 0 and b > 0:
            left = False
        if level == 0 and b < own // BLOCK - 1:
            right = False
        bias = jnp.zeros((1, keys), F32)
        if left is not False:
            bias = jnp.where(jnp.logical_and(col < BLOCK, left), MASKED, bias)
        if right is not False:
            bias = jnp.where(jnp.logical_and(col >= keys - BLOCK, right), MASKED, bias)
        return bias

    saved = []
    peaks, dens, nums = [], [], []
    for level, b in jobs:
        rows = BLOCK if level == 0 else queries[level].shape[0]
        query = split(stack_heads(queries[level][b * rows : (b + 1) * rows], heads))
        key = split(keys_of(level, b, (k_ref, k_s)))
        value = split(keys_of(level, b, (v_ref, v_s)))
        scores = mm(query, key, NT) + bias_of(level, b)
        peak = jnp.max(scores, axis=1, keepdims=True)
        weights = jnp.exp(scores - peak)
        den = jnp.sum(weights, axis=1, keepdims=True)
        halves = split(weights)
        num = unstack(mm(halves, value, NN), heads, width)
        saved.append((query, key, value, weights, halves))
        peaks.append(unstack(peak, heads, width))
        dens.append(unstack(den, heads, width))
        nums.append(num)
    blocks = own // BLOCK
    join = lambda parts: [jnp.concatenate(parts[:blocks])] + parts[blocks:]
    peaks, dens, nums = join(peaks), join(dens), join(nums)
    wide_peaks = [expand(buf, p, 2**l) for l, p in enumerate(peaks)]
    top = functools.reduce(jnp.maximum, wide_peaks)
    factors = [2.0**l * jnp.exp(p - top) for l, p in enumerate(wide_peaks)]
    num = sum(f * expand(buf, n, 2**l) for l, (f, n) in enumerate(zip(factors, nums)))
    den = sum(f * expand(buf, n, 2**l) for l, (f, n) in enumerate(zip(factors, dens)))
    inverse = 1.0 / den
    attended = num * inverse
    att = split(attended)

    d_att = d_ref[...]
    for side, c in sides:
        dw_ref[3, c] = mm(att, (gh_ref[side], gl_ref[side]), TN) * scale
    for target, (_, c) in zip((mine_ref, theirs_ref), sides):
        target[2 * near :] = mm(att, weight(3, c), NN)

    r = lax.broadcasted_iota(jnp.int32, (width, width), 0) // HEAD_DIM
    s = lax.broadcasted_iota(jnp.int32, (width, width), 1) // HEAD_DIM
    ones = jnp.where(r == s, 1.0, 0.0).astype(BF16)
    prod = d_att * attended
    p0, p1 = split(prod)
    delta = lax.dot_general(p0, ones, (NN, ((), ())), preferred_element_type=F32)
    delta = delta + lax.dot_general(p1, ones, (NN, ((), ())), preferred_element_type=F32)

    dk_s[...] = jnp.zeros_like(dk_s)
    dv_s[...] = jnp.zeros_like(dv_s)
    d_query = jnp.zeros((own, width), F32)
    level_dq = [[] for _ in range(LEVELS + 1)]
    for (level, b), (query, key, value, weights, halves) in zip(jobs, saved):
        if b == 0:
            share = factors[level] * inverse
            d_num = pool(buf, share * d_att, 2**level)
            d_den = pool(buf, -share * delta, 2**level)
        rows = BLOCK if level == 0 else d_num.shape[0]
        part = slice(b * rows, (b + 1) * rows)
        grad = split(stack_heads(d_num[part], heads))
        d_scores = split(weights * (mm(grad, value, NT) + stack_column(d_den[part], heads)))
        d_value = mm(halves, grad, TN)
        d_key = mm(d_scores, query, TN)
        level_dq[level].append(unstack(mm(d_scores, key, NN), heads, width))
        for ref, grads in ((dk_s, d_key), (dv_s, d_value)):
            if level == 0:
                start = own - BLOCK + b * BLOCK
                ref[start : start + 3 * BLOCK] += grads
            elif level == 1:
                ref[:own] += expand(buf, 0.5 * grads[:BLOCK], 2)
                ref[2 * own : 3 * own] += expand(buf, 0.5 * grads[BLOCK:], 2)
            else:
                start = 3 * own + (level - 2) * 2 * BLOCK
                ref[start : start + 2 * BLOCK] += grads
    for level, parts in enumerate(level_dq):
        d_query = d_query + expand(buf, jnp.concatenate(parts) * 2.0**-level, 2**level)
    dq = split(d_query * HEAD_DIM ** (-0.5))
    dk = split(dk_s[...])
    dv = split(dv_s[...])
    def near_rows(side, rows):
        return xh_ref[side, rows], xl_ref[side, rows]

    every = slice(None)
    for side, c in sides:
        dw_ref[0, c] = mm(near_rows(side, slice(own, 2 * own)), dq, TN) * scale
        for k, grads in ((1, dk), (2, dv)):
            dw_ref[k, c] = scale * (
                mm(near_rows(side, every), cut(grads, slice(near)), TN)
                + mm(far_rows(side), cut(grads, slice(near, near + far)), TN)
            )
    here = kept_left(place, core)
    for target, (side, c) in zip((mine_ref, theirs_ref), sides):
        target[near : 2 * near] = jnp.zeros((near, width), F32)
        beside = {}
        for start in range(0, near + far, own):
            rows = slice(start, start + own)
            dx = mm(cut(dk, rows), weight(1, c), NT) + mm(cut(dv, rows), weight(2, c), NT)
            if start == own:
                target[2 * own : near] = dx + mm(dq, weight(0, c), NT)
            elif start < near:
                beside[start] = dx
            else:
                for j in range(2):
                    part = dx[j * BLOCK : (j + 1) * BLOCK]
                    if start == near:
                        target[pl.ds(window(level_2[j], near), BLOCK)] += part
                    else:
                        at = pl.ds(window(level_3[j], near), 2 * BLOCK)
                        target[at] += expand(buf, 0.5 * part, 2)
        left, right = beside[0], beside[2 * own]
        mine_ref[side * own : (side + 1) * own] = jnp.where(here, left, right)
        theirs_ref[(1 - side) * own : (2 - side) * own] = jnp.where(here, right, left)


def attend(place, xs, known, count, scale):
    half = xs[0].shape[1]
    own, width = known[6].shape
    total = 3 * own + 4 * BLOCK
    rows = 7 * own
    vmem = pl.BlockSpec(memory_space=pltpu.VMEM)

    def shape(*s):
        return jax.ShapeDtypeStruct(s, F32)

    return pl.pallas_call(
        functools.partial(attend_kernel, count=count, scale=scale),
        out_shape=(shape(rows, half), shape(rows, half), shape(4, 2, half, width)),
        in_specs=[pl.BlockSpec(memory_space=pltpu.SMEM)] + [vmem] * 14,
        out_specs=(vmem,) * 3,
        scratch_shapes=[
            pltpu.VMEM((4 * BLOCK, width), F32),
            pltpu.VMEM((4 * BLOCK, width), F32),
            pltpu.VMEM((total, width), F32),
            pltpu.VMEM((total, width), F32),
            pltpu.VMEM((2, 4 * BLOCK, half), BF16),
            pltpu.VMEM((2, 4 * BLOCK, half), BF16),
            pltpu.VMEM((width // 128, own, 128), F32),
            pltpu.VMEM((3 * own, half), F32),
        ],
        compiler_params=pltpu.CompilerParams(vmem_limit_bytes=40 * 2**20),
        cost_estimate=pl.CostEstimate(
            flops=9 * 10**9, bytes_accessed=16 * 2**20, transcendentals=10**6
        ),
    )(place, *xs, *known)


def pool_kernel(x_ref, out_ref, buf):
    rows = 0.25 * pool(buf, x_ref[...], 4)
    for j in range(out_ref.shape[0]):
        out_ref[j] = rows


def pool_tokens(tokens, copies):
    own, half = tokens.shape
    return pl.pallas_call(
        pool_kernel,
        out_shape=jax.ShapeDtypeStruct((copies, own // 4, half), F32),
        scratch_shapes=[pltpu.VMEM((half // 128, own, 128), F32)],
    )(tokens)


CTX = ("x", "y", "z")
WIDE = ("x", "y")
LINE = ("z",)
SWAP = [(0, 1), (1, 0)]


def reverse(pairs):
    return [(j, i) for i, j in pairs]


def routes(count):
    lines = [(i, i + 8) if i % 8 < 4 else (i + 8, i) for i in range(count - 8)]
    even = [(i, i + 1) for i in range(0, count, 2)]
    odd = [(i, i + 1) for i in range(1, count - 1, 2)]
    beside = [(2 * i, 2 * j) for i, j in even + reverse(even)]
    beside = beside + [(2 * i + 1, 2 * j + 1) for i, j in odd + reverse(odd)]
    return lines, beside


def local(tokens, w_query, w_key, w_value, w_out, grad_out):
    count = lax.axis_size(CTX)
    place = lax.axis_index(CTX)
    core = lax.axis_index("head")
    own, half = tokens.shape
    quarter = own // 4
    near_rows = 3 * own
    low = place % 8 < 4
    lines, beside = routes(count)

    def swap(rows):
        return lax.ppermute(rows, "head", SWAP)

    def both_beside(rows):
        return lax.ppermute(rows, CTX + ("head",), beside)

    theirs = swap(tokens)
    line = lax.all_to_all(pool_tokens(tokens, 8), LINE, 0, 0).reshape(2, own, half)
    got = lax.ppermute(jnp.where(low, line[1], line[0]), CTX, lines)
    line = line.reshape(2 * own, half)
    late, _ = lax.optimization_barrier((jnp.stack([tokens, theirs]), line))
    close = both_beside(late)
    close, got = lax.optimization_barrier((close, got))
    where = jnp.stack([place, core]).astype(jnp.int32)
    xs = [tokens, grad_out, close, theirs, swap(grad_out), swap(close)]
    known = near(where, xs, (w_query, w_key, w_value, w_out))
    scale = (own * count) ** (-0.5)
    xs = [got, line, swap(got), swap(line)]
    mine, theirs, dw = attend(where, xs, known, count, scale)

    wide = lax.axis_size(WIDE)
    both = mine + swap(theirs)
    sizes = [2 * own, own, own, 2 * own]
    close, middle, got, line, layer_out = jnp.split(
        both, [sum(sizes[: i + 1]) for i in range(len(sizes))]
    )
    part = lax.all_to_all(dw.reshape(wide, -1, half), WIDE, 0, 0)
    got = lax.ppermute(got, CTX, reverse(lines))
    close = both_beside(close.reshape(2, own, half))
    part, got, close = lax.optimization_barrier((part, got, close))
    line = line.reshape(2, own, half)
    line = line + jnp.stack([jnp.where(low, 0.0, got), jnp.where(low, got, 0.0)])
    chunk = lax.all_to_all(part.sum(0).reshape(8, -1, half), LINE, 0, 0)
    chunk = spread(chunk.sum(0), LINE, 8).reshape(-1, half)
    chunk, line = lax.optimization_barrier((chunk, line))
    pooled = line.reshape(4, 2, quarter, half)
    for k in (1, 2, 4):
        upper = place // k % 2 == 1
        sent = jnp.where(upper, pooled[:, 0], pooled[:, 1])
        pooled = jnp.where(upper, pooled[:, 1], pooled[:, 0])
        pooled = pooled + lax.ppermute(sent, CTX, [(i, i ^ k) for i in range(count)])
        if k < 4:
            pooled = pooled.reshape(2 // k, 2, quarter, half)
    pooled = pooled[0]
    dw = spread(chunk, WIDE, wide).reshape(4, 2 * half, half)
    pooled = jnp.broadcast_to(0.25 * pooled[:, None], (quarter, 4, half)).reshape(own, half)
    grad_tokens = middle + close[0] + swap(close[1]) + pooled
    return (
        layer_out,
        grad_tokens,
        dw[0],
        dw[1],
        dw[2],
        jnp.concatenate([dw[3, :half], dw[3, half:]], axis=1),
    )


def spread(rows, axes, parts):
    return lax.all_to_all(jnp.broadcast_to(rows[None], (parts,) + rows.shape), axes, 0, 0)


def solution(mesh):
    lines = mesh.shape["ctx"] // 8
    split_mesh = jax.sharding.Mesh(
        mesh.devices.reshape(-(-lines // 4), min(lines, 4), 8, 2), ("x", "y", "z", "head")
    )
    placed = (
        P(CTX, "head"),
        P(None, "head"),
        P(None, "head"),
        P(None, "head"),
        P("head", None),
        P(CTX, "head"),
    )
    return jax.shard_map(
        local,
        mesh=split_mesh,
        in_specs=placed,
        out_specs=(P(CTX, "head"),) * 2 + (P(None, "head"),) * 3 + (P("head", None),),
        check_vma=False,
    )
```

```python
import functools
import jax
import jax.numpy as jnp
from jax import lax
from jax.experimental import pallas as pl
from jax.experimental.pallas import tpu as pltpu
from jax.sharding import PartitionSpec as P

HEAD_DIM = 64
BLOCK = 128
LEVELS = 3
F32 = jnp.float32
BF16 = jnp.bfloat16
MASKED = -1e30

NN = ((1,), (0,))
NT = ((1,), (1,))
TN = ((0,), (0,))


def split(value):
    high = value.astype(BF16)
    return high, (value - high.astype(F32)).astype(BF16)


def mm(a, b, dims):
    def dot(u, v):
        return lax.dot_general(u, v, (dims, ((), ())), preferred_element_type=F32)

    return dot(a[0], b[0]) + (dot(a[0], b[1]) + dot(a[1], b[0]))


def cut(pair, rows):
    return pair[0][rows], pair[1][rows]


def head_masks(rows, width, heads, dtype=F32):
    lane = lax.broadcasted_iota(jnp.int32, (rows, width), 1) // HEAD_DIM
    return [lane == h for h in range(heads)]


def stack_heads(value, heads):
    masks = head_masks(value.shape[0], value.shape[1], heads)
    return jnp.concatenate([jnp.where(m, value, 0.0) for m in masks], axis=0)


def unstack(value, heads, width):
    rows = value.shape[0] // heads
    masks = head_masks(rows, width, heads)
    out = jnp.zeros((rows, width), F32)
    for h, m in enumerate(masks):
        out = jnp.where(m, value[h * rows : (h + 1) * rows], out)
    return out


def stack_column(value, heads):
    lane = lax.broadcasted_iota(jnp.int32, value.shape, 1)
    return jnp.concatenate(
        [
            jnp.sum(jnp.where(lane == h * HEAD_DIM, value, 0.0), axis=1, keepdims=True)
            for h in range(heads)
        ],
        axis=0,
    )


def expand(buf, value, times):
    if times == 1:
        return value
    rows = value.shape[0]
    for half in range(value.shape[1] // 128):
        for j in range(times):
            buf[half, pl.ds(j, rows, stride=times), :] = value[:, half * 128 : half * 128 + 128]
    return jnp.concatenate(
        [buf[half, : rows * times, :] for half in range(value.shape[1] // 128)], axis=1
    )


def pool(buf, value, times):
    if times == 1:
        return value
    rows = value.shape[0] // times
    parts = []
    for half in range(value.shape[1] // 128):
        buf[half, : value.shape[0], :] = value[:, half * 128 : half * 128 + 128]
        total = buf[half, pl.ds(0, rows, stride=times), :]
        for j in range(1, times):
            total = total + buf[half, pl.ds(j, rows, stride=times), :]
        parts.append(total)
    return jnp.concatenate(parts, axis=1)


def kept_left(place, core):
    return lax.rem(place, 2) != core


def near_kernel(place_ref, *refs):
    away_refs, (theirs_ref, go_other_ref, close_ref, close_other_ref) = refs[:6], refs[6:10]
    wh_ref, wl_ref, xh_ref, xl_ref, gh_ref, gl_ref, q_ref, k_ref, v_ref, d_ref = refs[10:20]
    here_refs, sems = refs[20:26], refs[26]
    core = place_ref[1]
    own, width = q_ref.shape
    copies = [
        pltpu.make_async_copy(away, ref, sems.at[j])
        for j, (away, ref) in enumerate(zip(away_refs, here_refs))
    ]
    for copy in copies:
        copy.start()
    here = kept_left(place_ref[0], core)
    for side in range(2):
        kept, other = close_ref[side], close_other_ref[1 - side]
        left = jnp.where(here, kept, other)
        right = jnp.where(here, other, kept)
        xh_ref[side, :own], xl_ref[side, :own] = split(left)
        xh_ref[side, 2 * own :], xl_ref[side, 2 * own :] = split(right)
    middle = slice(own, 2 * own)
    xh_ref[1, middle], xl_ref[1, middle] = split(theirs_ref[...])
    for copy in copies:
        copy.wait()
    tokens_ref, go_ref, *w_refs = here_refs
    xh_ref[0, middle], xl_ref[0, middle] = split(tokens_ref[...])
    gh_ref[0], gl_ref[0] = split(go_ref[...])
    gh_ref[1], gl_ref[1] = split(go_other_ref[...])
    for c in range(2):
        for k, w_ref in enumerate(w_refs[:3]):
            wh_ref[k, c], wl_ref[k, c] = split(w_ref[c * width : (c + 1) * width])
        wh_ref[3, c], wl_ref[3, c] = split(w_refs[3][:, c * width : (c + 1) * width])

    def weight(k, c):
        return wh_ref[k, c], wl_ref[k, c]

    def project(k, start):
        rows = slice(start, start + own)
        return mm((xh_ref[0, rows], xl_ref[0, rows]), weight(k, core), NN) + mm(
            (xh_ref[1, rows], xl_ref[1, rows]), weight(k, 1 - core), NN
        )

    q_ref[...] = project(0, own) * HEAD_DIM ** (-0.5)
    for start in range(0, 3 * own, own):
        k_ref[start : start + own] = project(1, start)
        v_ref[start : start + own] = project(2, start)
    d_ref[...] = mm((gh_ref[0], gl_ref[0]), weight(3, core), NT) + mm(
        (gh_ref[1], gl_ref[1]), weight(3, 1 - core), NT
    )


def near(place, xs, weights):
    own, half = xs[0].shape
    width = weights[0].shape[1]
    vmem = pl.BlockSpec(memory_space=pltpu.VMEM)

    def shape(kind, *s):
        return jax.ShapeDtypeStruct(s, kind)

    return pl.pallas_call(
        near_kernel,
        out_shape=(
            shape(BF16, 4, 2, half, width),
            shape(BF16, 4, 2, half, width),
            shape(BF16, 2, 3 * own, half),
            shape(BF16, 2, 3 * own, half),
            shape(BF16, 2, own, half),
            shape(BF16, 2, own, half),
            shape(F32, own, width),
            shape(F32, 3 * own, width),
            shape(F32, 3 * own, width),
            shape(F32, own, width),
        ),
        in_specs=[pl.BlockSpec(memory_space=pltpu.SMEM)] + [pl.BlockSpec(memory_space=pltpu.HBM)] * 6 + [vmem] * 4,
        out_specs=(vmem,) * 10,
        scratch_shapes=[pltpu.VMEM(x.shape, F32) for x in (*xs[:2], *weights)]
        + [pltpu.SemaphoreType.DMA((6,))],
        compiler_params=pltpu.CompilerParams(vmem_limit_bytes=24 * 2**20),
        cost_estimate=pl.CostEstimate(
            flops=3 * 10**9, bytes_accessed=10 * 2**20, transcendentals=0
        ),
    )(place, *xs[:2], *weights, *xs[2:])


def attend_kernel(
    place_ref, *refs, count, scale,
):
    others_ref, group_ref, group_other_ref = refs[:3]
    pair_refs = refs[3:5]
    wh_ref, wl_ref, xh_ref, xl_ref, gh_ref, gl_ref, q_ref, k_ref, v_ref, d_ref = refs[5:15]
    mine_refs, theirs_refs, dw_ref = refs[15:17], refs[17:19], refs[19]
    k_s, v_s, dk_s, dv_s, xh_s, xl_s, buf = refs[20:]
    own, width = q_ref.shape
    near = 3 * own
    far = 4 * BLOCK
    heads = width // HEAD_DIM
    place = place_ref[0]
    core = place_ref[1]
    line = lax.rem(place, 8)
    edge = jnp.logical_or(place < 4, place >= count - 4)
    over = jnp.logical_or(line < 2, line >= 6)
    sides = ((0, core), (1, 1 - core))

    first = core == 0
    for side, pair_ref in enumerate(pair_refs):
        kept, other = group_ref[side], group_other_ref[1 - side]
        inline, cross = jnp.where(first, kept, other), jnp.where(first, other, kept)
        for j, part in enumerate((others_ref[side], pair_ref[...], inline, cross)):
            rows = slice(j * BLOCK, (j + 1) * BLOCK)
            xh_s[side, rows], xl_s[side, rows] = split(part)

    def weight(k, c):
        return wh_ref[k, c], wl_ref[k, c]

    def far_rows(side, rows=slice(None)):
        return xh_s[side, rows], xl_s[side, rows]

    for start in range(0, far, own):
        rows = slice(start, start + own)
        for k, ref in ((1, k_s), (2, v_s)):
            ref[rows] = sum(mm(far_rows(s, rows), weight(k, c), NN) for s, c in sides)

    jobs = []
    for b in range(own // BLOCK):
        jobs.append((0, b))
    for level in range(1, LEVELS + 1):
        jobs.append((level, 0))
    queries = [q_ref[...]]
    for level in range(1, LEVELS + 1):
        queries.append(pool(buf, q_ref[...], 2**level) * 2.0**-level)

    def keys_of(level, b, ref):
        if level == 0:
            start = own - BLOCK + b * BLOCK
            return ref[0][start : start + 3 * BLOCK]
        if level == 1:
            return jnp.concatenate(
                [0.5 * pool(buf, ref[0][:own], 2), 0.5 * pool(buf, ref[0][2 * own :], 2)]
            )
        start = (level - 2) * 2 * BLOCK
        return ref[1][start : start + 2 * BLOCK]

    def bias_of(level, b):
        keys = 3 * BLOCK if level == 0 else 2 * BLOCK
        col = lax.broadcasted_iota(jnp.int32, (1, keys), 1)
        left, right = place < 1, place >= count - 1
        if level > 1:
            left, right = False, jnp.logical_and(edge, over) if level == 2 else edge
        if level == 0 and b > 0:
            left = False
        if level == 0 and b < own // BLOCK - 1:
            right = False
        bias = jnp.zeros((1, keys), F32)
        if left is not False:
            bias = jnp.where(jnp.logical_and(col < BLOCK, left), MASKED, bias)
        if right is not False:
            bias = jnp.where(jnp.logical_and(col >= keys - BLOCK, right), MASKED, bias)
        return bias

    saved = []
    peaks, dens, nums = [], [], []
    for level, b in jobs:
        rows = BLOCK if level == 0 else queries[level].shape[0]
        query = split(stack_heads(queries[level][b * rows : (b + 1) * rows], heads))
        key = split(keys_of(level, b, (k_ref, k_s)))
        value = split(keys_of(level, b, (v_ref, v_s)))
        scores = mm(query, key, NT) + bias_of(level, b)
        peak = jnp.max(scores, axis=1, keepdims=True)
        weights = jnp.exp(scores - peak)
        den = jnp.sum(weights, axis=1, keepdims=True)
        halves = split(weights)
        num = unstack(mm(halves, value, NN), heads, width)
        saved.append((query, key, value, weights, halves))
        peaks.append(unstack(peak, heads, width))
        dens.append(unstack(den, heads, width))
        nums.append(num)
    blocks = own // BLOCK
    join = lambda parts: [jnp.concatenate(parts[:blocks])] + parts[blocks:]
    peaks, dens, nums = join(peaks), join(dens), join(nums)
    wide_peaks = [expand(buf, p, 2**l) for l, p in enumerate(peaks)]
    top = functools.reduce(jnp.maximum, wide_peaks)
    factors = [2.0**l * jnp.exp(p - top) for l, p in enumerate(wide_peaks)]
    num = sum(f * expand(buf, n, 2**l) for l, (f, n) in enumerate(zip(factors, nums)))
    den = sum(f * expand(buf, n, 2**l) for l, (f, n) in enumerate(zip(factors, dens)))
    inverse = 1.0 / den
    attended = num * inverse
    att = split(attended)

    d_att = d_ref[...]
    for side, c in sides:
        dw_ref[3, c] = mm(att, (gh_ref[side], gl_ref[side]), TN) * scale
    for (target, _), (_, c) in zip((mine_refs, theirs_refs), sides):
        target[near:] = mm(att, weight(3, c), NN)

    r = lax.broadcasted_iota(jnp.int32, (width, width), 0) // HEAD_DIM
    s = lax.broadcasted_iota(jnp.int32, (width, width), 1) // HEAD_DIM
    ones = jnp.where(r == s, 1.0, 0.0).astype(BF16)
    prod = d_att * attended
    p0, p1 = split(prod)
    delta = lax.dot_general(p0, ones, (NN, ((), ())), preferred_element_type=F32)
    delta = delta + lax.dot_general(p1, ones, (NN, ((), ())), preferred_element_type=F32)

    dk_s[...] = jnp.zeros_like(dk_s)
    dv_s[...] = jnp.zeros_like(dv_s)
    d_query = jnp.zeros((own, width), F32)
    level_dq = [[] for _ in range(LEVELS + 1)]
    for (level, b), (query, key, value, weights, halves) in zip(jobs, saved):
        if b == 0:
            share = factors[level] * inverse
            d_num = pool(buf, share * d_att, 2**level)
            d_den = pool(buf, -share * delta, 2**level)
        rows = BLOCK if level == 0 else d_num.shape[0]
        part = slice(b * rows, (b + 1) * rows)
        grad = split(stack_heads(d_num[part], heads))
        d_scores = split(weights * (mm(grad, value, NT) + stack_column(d_den[part], heads)))
        d_value = mm(halves, grad, TN)
        d_key = mm(d_scores, query, TN)
        level_dq[level].append(unstack(mm(d_scores, key, NN), heads, width))
        for ref, grads in ((dk_s, d_key), (dv_s, d_value)):
            if level == 0:
                start = own - BLOCK + b * BLOCK
                ref[start : start + 3 * BLOCK] += grads
            elif level == 1:
                ref[:own] += expand(buf, 0.5 * grads[:BLOCK], 2)
                ref[2 * own : 3 * own] += expand(buf, 0.5 * grads[BLOCK:], 2)
            else:
                start = 3 * own + (level - 2) * 2 * BLOCK
                ref[start : start + 2 * BLOCK] += grads
    for level, parts in enumerate(level_dq):
        d_query = d_query + expand(buf, jnp.concatenate(parts) * 2.0**-level, 2**level)
    dq = split(d_query * HEAD_DIM ** (-0.5))
    dk = split(dk_s[...])
    dv = split(dv_s[...])
    def near_rows(side, rows):
        return xh_ref[side, rows], xl_ref[side, rows]

    every = slice(None)
    for side, c in sides:
        dw_ref[0, c] = mm(near_rows(side, slice(own, 2 * own)), dq, TN) * scale
        for k, grads in ((1, dk), (2, dv)):
            dw_ref[k, c] = scale * (
                mm(near_rows(side, every), cut(grads, slice(near)), TN)
                + mm(far_rows(side), cut(grads, slice(near, near + far)), TN)
            )
    odd = lax.rem(place, 2) == 1
    for (target, far_target), (_, c) in zip((mine_refs, theirs_refs), sides):
        near_dx = []
        for start in range(0, near + far, own):
            rows = slice(start, start + own)
            dx = mm(cut(dk, rows), weight(1, c), NT) + mm(cut(dv, rows), weight(2, c), NT)
            if start == own:
                dx = dx + mm(dq, weight(0, c), NT)
            near_dx.append(dx)
            if start == 2 * own:
                left, _, right = near_dx
                target[:own] = jnp.where(odd, left, right)
                target[rows] = jnp.where(odd, right, left)
            elif start == own:
                target[rows] = dx
            elif start > own:
                far_target[start - near : start - near + own] = dx


def attend(place, xs, known, count, scale):
    half = xs[3].shape[1]
    own, width = known[6].shape
    total = 3 * own + 4 * BLOCK
    rows = 4 * own
    far = 4 * BLOCK
    vmem = pl.BlockSpec(memory_space=pltpu.VMEM)

    def shape(*s):
        return jax.ShapeDtypeStruct(s, F32)

    return pl.pallas_call(
        functools.partial(attend_kernel, count=count, scale=scale),
        out_shape=(
            shape(rows, half),
            shape(far, half),
            shape(rows, half),
            shape(far, half),
            shape(4, 2, half, width),
        ),
        in_specs=[pl.BlockSpec(memory_space=pltpu.SMEM)] + [vmem] * 15,
        out_specs=(vmem,) * 5,
        scratch_shapes=[
            pltpu.VMEM((4 * BLOCK, width), F32),
            pltpu.VMEM((4 * BLOCK, width), F32),
            pltpu.VMEM((total, width), F32),
            pltpu.VMEM((total, width), F32),
            pltpu.VMEM((2, 4 * BLOCK, half), BF16),
            pltpu.VMEM((2, 4 * BLOCK, half), BF16),
            pltpu.VMEM((width // 128, own, 128), F32),
        ],
        compiler_params=pltpu.CompilerParams(vmem_limit_bytes=40 * 2**20),
        cost_estimate=pl.CostEstimate(
            flops=9 * 10**9, bytes_accessed=16 * 2**20, transcendentals=10**6
        ),
    )(place, *xs, *known)


def pool_kernel(own_ref, other_ref, raw_ref, pooled_ref, buf):
    for side, ref in enumerate((own_ref, other_ref)):
        rows = ref[...]
        raw_ref[side] = rows
        pooled_ref[side] = 0.25 * pool(buf, rows, 4)


def pool_tokens(tokens, theirs):
    own, half = tokens.shape
    return pl.pallas_call(
        pool_kernel,
        out_shape=(
            jax.ShapeDtypeStruct((2, own, half), F32),
            jax.ShapeDtypeStruct((2, own // 4, half), F32),
        ),
        scratch_shapes=[pltpu.VMEM((half // 128, own, 128), F32)],
    )(tokens, theirs)


def arrange_kernel(
    place_ref, own_ref, far_ref, far_other_ref, close_ref, close_other_ref,
    pair_ref, others_ref, coarse_ref, buf,
):
    half = BLOCK // 2
    first = place_ref[1] == 0
    for side in range(2):
        far, far_other = far_ref[side], far_other_ref[1 - side]
        two, three = jnp.where(first, far, far_other), jnp.where(first, far_other, far)
        one = jnp.where(first, close_ref[side], close_other_ref[1 - side])
        one = 0.25 * pool(buf, one, 4)
        if side == 0:
            pair_ref[:half] = own_ref[0]
            pair_ref[half:] = one
        others_ref[side, :half] = two
        others_ref[side, half:] = three
        for j, rows in enumerate((own_ref[side], one, two, three)):
            coarse_ref[side, j * half // 2 : (j + 1) * half // 2] = 0.5 * pool(buf, rows, 2)


def arrange(place, pooled, far, far_other, close, close_other):
    own, half = close.shape[1:]
    vmem = pl.BlockSpec(memory_space=pltpu.VMEM)

    def shape(*s):
        return jax.ShapeDtypeStruct(s, F32)

    return pl.pallas_call(
        arrange_kernel,
        out_shape=(shape(BLOCK, half), shape(2, BLOCK, half), shape(2, BLOCK, half)),
        in_specs=[pl.BlockSpec(memory_space=pltpu.SMEM)] + [vmem] * 5,
        out_specs=(vmem,) * 3,
        scratch_shapes=[pltpu.VMEM((half // 128, own, 128), F32)],
    )(place, pooled, far, far_other, close, close_other)


def gather_kernel(own_ref, out_ref, got_ref, pair_ref, inline_ref, total_ref, buf):
    half = BLOCK // 2
    total = own_ref[...] + out_ref[...] + got_ref[half + half // 2 :]
    total = total + expand(buf, 0.25 * (pair_ref[:half] + got_ref[:half]), 4)
    coarse = inline_ref[: half // 2] + got_ref[half : half + half // 2]
    total_ref[...] = total + expand(buf, 0.125 * coarse, 8)


def gather_tokens(own, out, got, pair, inline):
    rows, half = own.shape
    return pl.pallas_call(
        gather_kernel,
        out_shape=jax.ShapeDtypeStruct((rows, half), F32),
        scratch_shapes=[pltpu.VMEM((half // 128, rows, 128), F32)],
    )(own, out, got, pair, inline)


CTX = ("x", "y", "z")
WIDE = ("x", "y")
SWAP = [(0, 1), (1, 0)]


def routes(count):
    beside = [(i, i + 1) for i in range(1, count - 1, 2)]
    mirror = [(i, i - i % 8 + 7 - i % 8) for i in range(count)]
    cross = [(i, i + 15 - 2 * (i % 8)) for i in range(count - 8) if i % 8 >= 4]
    pairs = [(i, 8 * ((i + 2) // 8) + 7 - i % 8) for i in range(count - 2) if i % 8 in (2, 3, 6, 7)]
    return [p + reverse(p) for p in (beside, cross, pairs)] + [mirror]


def reverse(pairs):
    return [(j, i) for i, j in pairs]


def local(tokens, w_query, w_key, w_value, w_out, grad_out):
    count = lax.axis_size(CTX)
    place = lax.axis_index(CTX)
    core = lax.axis_index("head")
    own, half = tokens.shape
    beside, across, pairs, mirror = routes(count)

    def send(rows, pairs):
        return lax.ppermute(rows, CTX, pairs)

    def xor(rows, k):
        return send(rows, [(i, i ^ k) for i in range(count)])

    def swap(rows):
        return lax.ppermute(rows, "head", SWAP)

    def by_core(rows, first, second):
        pairs = [(2 * i + c, 2 * j + c) for c, r in enumerate((first, second)) for i, j in r]
        return lax.ppermute(rows, CTX + ("head",), pairs)

    one, two, three = ([(i, i ^ k) for i in range(count)] for k in (1, 2, 3))
    where = jnp.stack([place, core]).astype(jnp.int32)
    theirs = swap(tokens)
    raw, pooled = pool_tokens(tokens, theirs)
    far, close = by_core(pooled, two, three), by_core(raw, one, beside)
    far, close = lax.optimization_barrier((far, close))
    far_other, close_other = swap(far), swap(close)
    pair, others, coarse = arrange(where, pooled, far, far_other, close, close_other)
    group = by_core(coarse, mirror, across)
    pair = send(pair, pairs)
    close_other, _ = lax.optimization_barrier((close_other, coarse))
    xs = [tokens, grad_out, theirs, swap(grad_out), close, close_other]
    known = near(where, xs, (w_query, w_key, w_value, w_out))
    group, pair, known = lax.optimization_barrier((group, pair, known))
    away = [others, group, swap(group), pair, swap(pair)]
    scale = (own * count) ** (-0.5)
    mine, far_mine, theirs, far_theirs, dw = attend(where, away, known, count, scale)

    wide = lax.axis_size(WIDE)
    others, pair, inline, cross = jnp.split(far_mine + swap(far_theirs), 4)
    one, middle, out, layer_out = jnp.split(mine + swap(theirs), 4)
    part = lax.all_to_all(dw.reshape(wide, -1, half), WIDE, 0, 0)
    pair, inline, cross = send(pair, pairs), send(inline, mirror), send(cross, across)
    part, pair, inline, cross, out = lax.optimization_barrier((part, pair, inline, cross, out))
    out = send(out, beside)
    chunk = part.sum(0)
    for k in (4, 2, 1):
        chunk = chunk + xor(chunk, k)
    chunk, pair, inline, cross, out = lax.optimization_barrier((chunk, pair, inline, cross, out))

    dw = spread(chunk, WIDE, wide).reshape(4, 2 * half, half)
    inline = inline + cross
    got = xor(jnp.concatenate([others, inline[64:]]), 2)
    pair, inline = pair + got[:BLOCK], inline[:64] + got[BLOCK:]
    got = xor(jnp.concatenate([pair[64:], inline[32:], one]), 1)
    grad_tokens = gather_tokens(middle, out, got, pair, inline)
    return (
        layer_out,
        grad_tokens,
        dw[0],
        dw[1],
        dw[2],
        jnp.concatenate([dw[3, :half], dw[3, half:]], axis=1),
    )


def spread(rows, axes, parts):
    return lax.all_to_all(jnp.broadcast_to(rows[None], (parts,) + rows.shape), axes, 0, 0)


def solution(mesh):
    lines = mesh.shape["ctx"] // 8
    split_mesh = jax.sharding.Mesh(
        mesh.devices.reshape(-(-lines // 4), min(lines, 4), 8, 2), ("x", "y", "z", "head")
    )
    placed = (
        P(CTX, "head"),
        P(None, "head"),
        P(None, "head"),
        P(None, "head"),
        P("head", None),
        P(CTX, "head"),
    )
    return jax.shard_map(
        local,
        mesh=split_mesh,
        in_specs=placed,
        out_specs=(P(CTX, "head"),) * 2 + (P(None, "head"),) * 3 + (P("head", None),),
        check_vma=False,
    )
```

```python
import functools
import jax
import jax.numpy as jnp
from jax import lax
from jax.experimental import pallas as pl
from jax.experimental.pallas import tpu as pltpu
from jax.sharding import PartitionSpec as P

HEAD_DIM = 64
BLOCK = 128
LEVELS = 3
F32 = jnp.float32
BF16 = jnp.bfloat16
MASKED = -1e30

NN = ((1,), (0,))
NT = ((1,), (1,))
TN = ((0,), (0,))


def split(value):
    high = value.astype(BF16)
    return high, (value - high.astype(F32)).astype(BF16)


def mm(a, b, dims):
    def dot(u, v):
        return lax.dot_general(u, v, (dims, ((), ())), preferred_element_type=F32)

    return dot(a[0], b[0]) + (dot(a[0], b[1]) + dot(a[1], b[0]))


def cut(pair, rows):
    return pair[0][rows], pair[1][rows]


def head_masks(rows, width, heads, dtype=F32):
    lane = lax.broadcasted_iota(jnp.int32, (rows, width), 1) // HEAD_DIM
    return [lane == h for h in range(heads)]


def stack_heads(value, heads):
    masks = head_masks(value.shape[0], value.shape[1], heads)
    return jnp.concatenate([jnp.where(m, value, 0.0) for m in masks], axis=0)


def unstack(value, heads, width):
    rows = value.shape[0] // heads
    masks = head_masks(rows, width, heads)
    out = jnp.zeros((rows, width), F32)
    for h, m in enumerate(masks):
        out = jnp.where(m, value[h * rows : (h + 1) * rows], out)
    return out


def stack_column(value, heads):
    lane = lax.broadcasted_iota(jnp.int32, value.shape, 1)
    return jnp.concatenate(
        [
            jnp.sum(jnp.where(lane == h * HEAD_DIM, value, 0.0), axis=1, keepdims=True)
            for h in range(heads)
        ],
        axis=0,
    )


def expand(buf, value, times):
    if times == 1:
        return value
    rows = value.shape[0]
    for half in range(value.shape[1] // 128):
        for j in range(times):
            buf[half, pl.ds(j, rows, stride=times), :] = value[:, half * 128 : half * 128 + 128]
    return jnp.concatenate(
        [buf[half, : rows * times, :] for half in range(value.shape[1] // 128)], axis=1
    )


def pool(buf, value, times):
    if times == 1:
        return value
    rows = value.shape[0] // times
    parts = []
    for half in range(value.shape[1] // 128):
        buf[half, : value.shape[0], :] = value[:, half * 128 : half * 128 + 128]
        total = buf[half, pl.ds(0, rows, stride=times), :]
        for j in range(1, times):
            total = total + buf[half, pl.ds(j, rows, stride=times), :]
        parts.append(total)
    return jnp.concatenate(parts, axis=1)


def kept_left(place, core):
    return lax.rem(place, 2) != core


def near_kernel(place_ref, *refs):
    away_refs, (theirs_ref, go_other_ref, close_ref, close_other_ref) = refs[:6], refs[6:10]
    wh_ref, wl_ref, xh_ref, xl_ref, gh_ref, gl_ref, q_ref, k_ref, v_ref, d_ref = refs[10:20]
    here_refs, sems = refs[20:26], refs[26]
    core = place_ref[1]
    own, width = q_ref.shape
    copies = [
        pltpu.make_async_copy(away, ref, sems.at[j])
        for j, (away, ref) in enumerate(zip(away_refs, here_refs))
    ]
    for copy in copies:
        copy.start()
    here = kept_left(place_ref[0], core)
    for side in range(2):
        kept, other = close_ref[side], close_other_ref[1 - side]
        left = jnp.where(here, kept, other)
        right = jnp.where(here, other, kept)
        xh_ref[side, :own], xl_ref[side, :own] = split(left)
        xh_ref[side, 2 * own :], xl_ref[side, 2 * own :] = split(right)
    middle = slice(own, 2 * own)
    xh_ref[1, middle], xl_ref[1, middle] = split(theirs_ref[...])
    for copy in copies:
        copy.wait()
    tokens_ref, go_ref, *w_refs = here_refs
    xh_ref[0, middle], xl_ref[0, middle] = split(tokens_ref[...])
    gh_ref[0], gl_ref[0] = split(go_ref[...])
    gh_ref[1], gl_ref[1] = split(go_other_ref[...])
    for c in range(2):
        for k, w_ref in enumerate(w_refs[:3]):
            wh_ref[k, c], wl_ref[k, c] = split(w_ref[c * width : (c + 1) * width])
        wh_ref[3, c], wl_ref[3, c] = split(w_refs[3][:, c * width : (c + 1) * width])

    def weight(k, c):
        return wh_ref[k, c], wl_ref[k, c]

    def project(k, start):
        rows = slice(start, start + own)
        return mm((xh_ref[0, rows], xl_ref[0, rows]), weight(k, core), NN) + mm(
            (xh_ref[1, rows], xl_ref[1, rows]), weight(k, 1 - core), NN
        )

    q_ref[...] = project(0, own) * HEAD_DIM ** (-0.5)
    for start in range(0, 3 * own, own):
        k_ref[start : start + own] = project(1, start)
        v_ref[start : start + own] = project(2, start)
    d_ref[...] = mm((gh_ref[0], gl_ref[0]), weight(3, core), NT) + mm(
        (gh_ref[1], gl_ref[1]), weight(3, 1 - core), NT
    )


def near(place, xs, weights):
    own, half = xs[0].shape
    width = weights[0].shape[1]
    vmem = pl.BlockSpec(memory_space=pltpu.VMEM)

    def shape(kind, *s):
        return jax.ShapeDtypeStruct(s, kind)

    return pl.pallas_call(
        near_kernel,
        out_shape=(
            shape(BF16, 4, 2, half, width),
            shape(BF16, 4, 2, half, width),
            shape(BF16, 2, 3 * own, half),
            shape(BF16, 2, 3 * own, half),
            shape(BF16, 2, own, half),
            shape(BF16, 2, own, half),
            shape(F32, own, width),
            shape(F32, 3 * own, width),
            shape(F32, 3 * own, width),
            shape(F32, own, width),
        ),
        in_specs=[pl.BlockSpec(memory_space=pltpu.SMEM)] + [pl.BlockSpec(memory_space=pltpu.HBM)] * 6 + [vmem] * 4,
        out_specs=(vmem,) * 10,
        scratch_shapes=[pltpu.VMEM(x.shape, F32) for x in (*xs[:2], *weights)]
        + [pltpu.SemaphoreType.DMA((6,))],
        compiler_params=pltpu.CompilerParams(vmem_limit_bytes=24 * 2**20),
        cost_estimate=pl.CostEstimate(
            flops=3 * 10**9, bytes_accessed=10 * 2**20, transcendentals=0
        ),
    )(place, *xs[:2], *weights, *xs[2:])


def attend_kernel(
    place_ref, *refs, count, scale,
):
    others_ref, group_ref, group_other_ref = refs[:3]
    pair_refs = refs[3:5]
    wh_ref, wl_ref, xh_ref, xl_ref, gh_ref, gl_ref, q_ref, k_ref, v_ref, d_ref = refs[5:15]
    mine_refs, theirs_refs, dw_ref = refs[15:17], refs[17:19], refs[19]
    k_s, v_s, dk_s, dv_s, xh_s, xl_s, buf = refs[20:]
    own, width = q_ref.shape
    near = 3 * own
    far = 4 * BLOCK
    heads = width // HEAD_DIM
    place = place_ref[0]
    core = place_ref[1]
    line = lax.rem(place, 8)
    edge = jnp.logical_or(place < 4, place >= count - 4)
    over = jnp.logical_or(line < 2, line >= 6)
    sides = ((0, core), (1, 1 - core))

    first = core == 0
    for side, pair_ref in enumerate(pair_refs):
        kept, other = group_ref[side], group_other_ref[1 - side]
        inline, cross = jnp.where(first, kept, other), jnp.where(first, other, kept)
        for j, part in enumerate((others_ref[side], pair_ref[...], inline, cross)):
            rows = slice(j * BLOCK, (j + 1) * BLOCK)
            xh_s[side, rows], xl_s[side, rows] = split(part)

    def weight(k, c):
        return wh_ref[k, c], wl_ref[k, c]

    def far_rows(side, rows=slice(None)):
        return xh_s[side, rows], xl_s[side, rows]

    for start in range(0, far, own):
        rows = slice(start, start + own)
        for k, ref in ((1, k_s), (2, v_s)):
            ref[rows] = sum(mm(far_rows(s, rows), weight(k, c), NN) for s, c in sides)

    jobs = []
    for b in range(own // BLOCK):
        jobs.append((0, b))
    for level in range(1, LEVELS + 1):
        jobs.append((level, 0))
    queries = [q_ref[...]]
    for level in range(1, LEVELS + 1):
        queries.append(pool(buf, q_ref[...], 2**level) * 2.0**-level)

    def keys_of(level, b, ref):
        if level == 0:
            start = own - BLOCK + b * BLOCK
            return ref[0][start : start + 3 * BLOCK]
        if level == 1:
            return jnp.concatenate(
                [0.5 * pool(buf, ref[0][:own], 2), 0.5 * pool(buf, ref[0][2 * own :], 2)]
            )
        start = (level - 2) * 2 * BLOCK
        return ref[1][start : start + 2 * BLOCK]

    def bias_of(level, b):
        keys = 3 * BLOCK if level == 0 else 2 * BLOCK
        col = lax.broadcasted_iota(jnp.int32, (1, keys), 1)
        left, right = place < 1, place >= count - 1
        if level > 1:
            left, right = False, jnp.logical_and(edge, over) if level == 2 else edge
        if level == 0 and b > 0:
            left = False
        if level == 0 and b < own // BLOCK - 1:
            right = False
        bias = jnp.zeros((1, keys), F32)
        if left is not False:
            bias = jnp.where(jnp.logical_and(col < BLOCK, left), MASKED, bias)
        if right is not False:
            bias = jnp.where(jnp.logical_and(col >= keys - BLOCK, right), MASKED, bias)
        return bias

    saved = []
    peaks, dens, nums = [], [], []
    for level, b in jobs:
        rows = BLOCK if level == 0 else queries[level].shape[0]
        query = split(stack_heads(queries[level][b * rows : (b + 1) * rows], heads))
        key = split(keys_of(level, b, (k_ref, k_s)))
        value = split(keys_of(level, b, (v_ref, v_s)))
        scores = mm(query, key, NT) + bias_of(level, b)
        peak = jnp.max(scores, axis=1, keepdims=True)
        weights = jnp.exp(scores - peak)
        den = jnp.sum(weights, axis=1, keepdims=True)
        halves = split(weights)
        num = unstack(mm(halves, value, NN), heads, width)
        saved.append((query, key, value, weights, halves))
        peaks.append(unstack(peak, heads, width))
        dens.append(unstack(den, heads, width))
        nums.append(num)
    blocks = own // BLOCK
    join = lambda parts: [jnp.concatenate(parts[:blocks])] + parts[blocks:]
    peaks, dens, nums = join(peaks), join(dens), join(nums)
    wide_peaks = [expand(buf, p, 2**l) for l, p in enumerate(peaks)]
    top = functools.reduce(jnp.maximum, wide_peaks)
    factors = [2.0**l * jnp.exp(p - top) for l, p in enumerate(wide_peaks)]
    num = sum(f * expand(buf, n, 2**l) for l, (f, n) in enumerate(zip(factors, nums)))
    den = sum(f * expand(buf, n, 2**l) for l, (f, n) in enumerate(zip(factors, dens)))
    inverse = 1.0 / den
    attended = num * inverse
    att = split(attended)

    d_att = d_ref[...]
    for side, c in sides:
        dw_ref[3, c] = mm(att, (gh_ref[side], gl_ref[side]), TN) * scale
    for (target, _), (_, c) in zip((mine_refs, theirs_refs), sides):
        target[near:] = mm(att, weight(3, c), NN)

    r = lax.broadcasted_iota(jnp.int32, (width, width), 0) // HEAD_DIM
    s = lax.broadcasted_iota(jnp.int32, (width, width), 1) // HEAD_DIM
    ones = jnp.where(r == s, 1.0, 0.0).astype(BF16)
    prod = d_att * attended
    p0, p1 = split(prod)
    delta = lax.dot_general(p0, ones, (NN, ((), ())), preferred_element_type=F32)
    delta = delta + lax.dot_general(p1, ones, (NN, ((), ())), preferred_element_type=F32)

    dk_s[...] = jnp.zeros_like(dk_s)
    dv_s[...] = jnp.zeros_like(dv_s)
    d_query = jnp.zeros((own, width), F32)
    level_dq = [[] for _ in range(LEVELS + 1)]
    for (level, b), (query, key, value, weights, halves) in zip(jobs, saved):
        if b == 0:
            share = factors[level] * inverse
            d_num = pool(buf, share * d_att, 2**level)
            d_den = pool(buf, -share * delta, 2**level)
        rows = BLOCK if level == 0 else d_num.shape[0]
        part = slice(b * rows, (b + 1) * rows)
        grad = split(stack_heads(d_num[part], heads))
        d_scores = split(weights * (mm(grad, value, NT) + stack_column(d_den[part], heads)))
        d_value = mm(halves, grad, TN)
        d_key = mm(d_scores, query, TN)
        level_dq[level].append(unstack(mm(d_scores, key, NN), heads, width))
        for ref, grads in ((dk_s, d_key), (dv_s, d_value)):
            if level == 0:
                start = own - BLOCK + b * BLOCK
                ref[start : start + 3 * BLOCK] += grads
            elif level == 1:
                ref[:own] += expand(buf, 0.5 * grads[:BLOCK], 2)
                ref[2 * own : 3 * own] += expand(buf, 0.5 * grads[BLOCK:], 2)
            else:
                start = 3 * own + (level - 2) * 2 * BLOCK
                ref[start : start + 2 * BLOCK] += grads
    for level, parts in enumerate(level_dq):
        d_query = d_query + expand(buf, jnp.concatenate(parts) * 2.0**-level, 2**level)
    dq = split(d_query * HEAD_DIM ** (-0.5))
    dk = split(dk_s[...])
    dv = split(dv_s[...])
    def near_rows(side, rows):
        return xh_ref[side, rows], xl_ref[side, rows]

    every = slice(None)
    for side, c in sides:
        dw_ref[0, c] = mm(near_rows(side, slice(own, 2 * own)), dq, TN) * scale
        for k, grads in ((1, dk), (2, dv)):
            dw_ref[k, c] = scale * (
                mm(near_rows(side, every), cut(grads, slice(near)), TN)
                + mm(far_rows(side), cut(grads, slice(near, near + far)), TN)
            )
    odd = lax.rem(place, 2) == 1
    for (target, far_target), (_, c) in zip((mine_refs, theirs_refs), sides):
        near_dx = []
        for start in range(0, near + far, own):
            rows = slice(start, start + own)
            dx = mm(cut(dk, rows), weight(1, c), NT) + mm(cut(dv, rows), weight(2, c), NT)
            if start == own:
                dx = dx + mm(dq, weight(0, c), NT)
            near_dx.append(dx)
            if start == 2 * own:
                left, _, right = near_dx
                target[:own] = jnp.where(odd, left, right)
                target[rows] = jnp.where(odd, right, left)
            elif start == own:
                target[rows] = dx
            elif start > own:
                far_target[start - near : start - near + own] = dx


def attend(place, xs, known, count, scale):
    half = xs[3].shape[1]
    own, width = known[6].shape
    total = 3 * own + 4 * BLOCK
    rows = 4 * own
    far = 4 * BLOCK
    vmem = pl.BlockSpec(memory_space=pltpu.VMEM)

    def shape(*s):
        return jax.ShapeDtypeStruct(s, F32)

    return pl.pallas_call(
        functools.partial(attend_kernel, count=count, scale=scale),
        out_shape=(
            shape(rows, half),
            shape(far, half),
            shape(rows, half),
            shape(far, half),
            shape(4, 2, half, width),
        ),
        in_specs=[pl.BlockSpec(memory_space=pltpu.SMEM)] + [vmem] * 15,
        out_specs=(vmem,) * 5,
        scratch_shapes=[
            pltpu.VMEM((4 * BLOCK, width), F32),
            pltpu.VMEM((4 * BLOCK, width), F32),
            pltpu.VMEM((total, width), F32),
            pltpu.VMEM((total, width), F32),
            pltpu.VMEM((2, 4 * BLOCK, half), BF16),
            pltpu.VMEM((2, 4 * BLOCK, half), BF16),
            pltpu.VMEM((width // 128, own, 128), F32),
        ],
        compiler_params=pltpu.CompilerParams(vmem_limit_bytes=40 * 2**20),
        cost_estimate=pl.CostEstimate(
            flops=9 * 10**9, bytes_accessed=16 * 2**20, transcendentals=10**6
        ),
    )(place, *xs, *known)


def pool_kernel(own_ref, other_ref, raw_ref, pooled_ref, buf):
    for side, ref in enumerate((own_ref, other_ref)):
        rows = ref[...]
        raw_ref[side] = rows
        pooled_ref[side] = 0.25 * pool(buf, rows, 4)


def pool_tokens(tokens, theirs):
    own, half = tokens.shape
    return pl.pallas_call(
        pool_kernel,
        out_shape=(
            jax.ShapeDtypeStruct((2, own, half), F32),
            jax.ShapeDtypeStruct((2, own // 4, half), F32),
        ),
        scratch_shapes=[pltpu.VMEM((half // 128, own, 128), F32)],
        compiler_params=pltpu.CompilerParams(vmem_limit_bytes=8 * 2**20),
    )(tokens, theirs)


def arrange_kernel(
    place_ref, own_ref, far_ref, far_other_ref, close_ref, close_other_ref,
    pair_ref, others_ref, coarse_ref, buf,
):
    half = BLOCK // 2
    first = place_ref[1] == 0
    for side in range(2):
        far, far_other = far_ref[side], far_other_ref[1 - side]
        two, three = jnp.where(first, far, far_other), jnp.where(first, far_other, far)
        one = jnp.where(first, close_ref[side], close_other_ref[1 - side])
        one = 0.25 * pool(buf, one, 4)
        if side == 0:
            pair_ref[:half] = own_ref[0]
            pair_ref[half:] = one
        others_ref[side, :half] = two
        others_ref[side, half:] = three
        for j, rows in enumerate((own_ref[side], one, two, three)):
            coarse_ref[side, j * half // 2 : (j + 1) * half // 2] = 0.5 * pool(buf, rows, 2)


def arrange(place, pooled, far, far_other, close, close_other):
    own, half = close.shape[1:]
    vmem = pl.BlockSpec(memory_space=pltpu.VMEM)

    def shape(*s):
        return jax.ShapeDtypeStruct(s, F32)

    return pl.pallas_call(
        arrange_kernel,
        out_shape=(shape(BLOCK, half), shape(2, BLOCK, half), shape(2, BLOCK, half)),
        in_specs=[pl.BlockSpec(memory_space=pltpu.SMEM)] + [vmem] * 5,
        out_specs=(vmem,) * 3,
        scratch_shapes=[pltpu.VMEM((half // 128, own, 128), F32)],
        compiler_params=pltpu.CompilerParams(vmem_limit_bytes=8 * 2**20),
    )(place, pooled, far, far_other, close, close_other)


def gather_kernel(own_ref, out_ref, got_ref, pair_ref, inline_ref, total_ref, buf):
    half = BLOCK // 2
    total = own_ref[...] + out_ref[...] + got_ref[half + half // 2 :]
    total = total + expand(buf, 0.25 * (pair_ref[:half] + got_ref[:half]), 4)
    coarse = inline_ref[: half // 2] + got_ref[half : half + half // 2]
    total_ref[...] = total + expand(buf, 0.125 * coarse, 8)


def gather_tokens(own, out, got, pair, inline):
    rows, half = own.shape
    return pl.pallas_call(
        gather_kernel,
        out_shape=jax.ShapeDtypeStruct((rows, half), F32),
        scratch_shapes=[pltpu.VMEM((half // 128, rows, 128), F32)],
        compiler_params=pltpu.CompilerParams(vmem_limit_bytes=8 * 2**20),
    )(own, out, got, pair, inline)


CTX = ("x", "y", "z")
WIDE = ("x", "y")
SWAP = [(0, 1), (1, 0)]


def routes(count):
    beside = [(i, i + 1) for i in range(1, count - 1, 2)]
    mirror = [(i, i - i % 8 + 7 - i % 8) for i in range(count)]
    cross = [(i, i + 15 - 2 * (i % 8)) for i in range(count - 8) if i % 8 >= 4]
    pairs = [(i, 8 * ((i + 2) // 8) + 7 - i % 8) for i in range(count - 2) if i % 8 in (2, 3, 6, 7)]
    return [p + reverse(p) for p in (beside, cross, pairs)] + [mirror]


def reverse(pairs):
    return [(j, i) for i, j in pairs]


def local(tokens, w_query, w_key, w_value, w_out, grad_out):
    count = lax.axis_size(CTX)
    place = lax.axis_index(CTX)
    core = lax.axis_index("head")
    own, half = tokens.shape
    beside, across, pairs, mirror = routes(count)

    def send(rows, pairs):
        return lax.ppermute(rows, CTX, pairs)

    def xor(rows, k):
        return send(rows, [(i, i ^ k) for i in range(count)])

    def swap(rows):
        return lax.ppermute(rows, "head", SWAP)

    def by_core(rows, first, second):
        pairs = [(2 * i + c, 2 * j + c) for c, r in enumerate((first, second)) for i, j in r]
        return lax.ppermute(rows, CTX + ("head",), pairs)

    one, two, three = ([(i, i ^ k) for i in range(count)] for k in (1, 2, 3))
    where = jnp.stack([place, core]).astype(jnp.int32)
    theirs = swap(tokens)
    raw, pooled = pool_tokens(tokens, theirs)
    far, close = by_core(pooled, two, three), by_core(raw, one, beside)
    far, close = lax.optimization_barrier((far, close))
    far_other, close_other = swap(far), swap(close)
    pair, others, coarse = arrange(where, pooled, far, far_other, close, close_other)
    group = by_core(coarse, mirror, across)
    pair = send(pair, pairs)
    close_other, _ = lax.optimization_barrier((close_other, coarse))
    xs = [tokens, grad_out, theirs, swap(grad_out), close, close_other]
    known = near(where, xs, (w_query, w_key, w_value, w_out))
    group, pair, known = lax.optimization_barrier((group, pair, known))
    away = [others, group, swap(group), pair, swap(pair)]
    scale = (own * count) ** (-0.5)
    mine, far_mine, theirs, far_theirs, dw = attend(where, away, known, count, scale)

    wide = lax.axis_size(WIDE)
    others, pair, inline, cross = jnp.split(far_mine + swap(far_theirs), 4)
    one, middle, out, layer_out = jnp.split(mine + swap(theirs), 4)
    part = lax.all_to_all(dw.reshape(wide, -1, half), WIDE, 0, 0)
    pair, inline, cross = send(pair, pairs), send(inline, mirror), send(cross, across)
    part, pair, inline, cross, out = lax.optimization_barrier((part, pair, inline, cross, out))
    out = send(out, beside)
    chunk = part.sum(0)
    for k in (4, 2, 1):
        chunk = chunk + xor(chunk, k)
    chunk, pair, inline, cross, out = lax.optimization_barrier((chunk, pair, inline, cross, out))

    dw = spread(chunk, WIDE, wide).reshape(4, 2 * half, half)
    inline = inline + cross
    got = xor(jnp.concatenate([others, inline[64:]]), 2)
    pair, inline = pair + got[:BLOCK], inline[:64] + got[BLOCK:]
    got = xor(jnp.concatenate([pair[64:], inline[32:], one]), 1)
    grad_tokens = gather_tokens(middle, out, got, pair, inline)
    return (
        layer_out,
        grad_tokens,
        dw[0],
        dw[1],
        dw[2],
        jnp.concatenate([dw[3, :half], dw[3, half:]], axis=1),
    )


def spread(rows, axes, parts):
    return lax.all_to_all(jnp.broadcast_to(rows[None], (parts,) + rows.shape), axes, 0, 0)


def solution(mesh):
    lines = mesh.shape["ctx"] // 8
    split_mesh = jax.sharding.Mesh(
        mesh.devices.reshape(-(-lines // 4), min(lines, 4), 8, 2), ("x", "y", "z", "head")
    )
    placed = (
        P(CTX, "head"),
        P(None, "head"),
        P(None, "head"),
        P(None, "head"),
        P("head", None),
        P(CTX, "head"),
    )
    return jax.shard_map(
        local,
        mesh=split_mesh,
        in_specs=placed,
        out_specs=(P(CTX, "head"),) * 2 + (P(None, "head"),) * 3 + (P("head", None),),
        check_vma=False,
    )
```

```python
import functools
import jax
import jax.numpy as jnp
from jax import lax
from jax.experimental import pallas as pl
from jax.experimental.pallas import tpu as pltpu
from jax.sharding import PartitionSpec as P

HEAD_DIM = 64
BLOCK = 128
LEVELS = 3
F32 = jnp.float32
BF16 = jnp.bfloat16
MASKED = -1e30

NN = ((1,), (0,))
NT = ((1,), (1,))
TN = ((0,), (0,))


def split(value):
    high = value.astype(BF16)
    return high, (value - high.astype(F32)).astype(BF16)


def mm(a, b, dims):
    def dot(u, v):
        return lax.dot_general(u, v, (dims, ((), ())), preferred_element_type=F32)

    return dot(a[0], b[0]) + (dot(a[0], b[1]) + dot(a[1], b[0]))


def cut(pair, rows):
    return pair[0][rows], pair[1][rows]


def head_masks(rows, width, heads, dtype=F32):
    lane = lax.broadcasted_iota(jnp.int32, (rows, width), 1) // HEAD_DIM
    return [lane == h for h in range(heads)]


def stack_heads(value, heads):
    masks = head_masks(value.shape[0], value.shape[1], heads)
    return jnp.concatenate([jnp.where(m, value, 0.0) for m in masks], axis=0)


def unstack(value, heads, width):
    rows = value.shape[0] // heads
    masks = head_masks(rows, width, heads)
    out = jnp.zeros((rows, width), F32)
    for h, m in enumerate(masks):
        out = jnp.where(m, value[h * rows : (h + 1) * rows], out)
    return out


def stack_column(value, heads):
    lane = lax.broadcasted_iota(jnp.int32, value.shape, 1)
    return jnp.concatenate(
        [
            jnp.sum(jnp.where(lane == h * HEAD_DIM, value, 0.0), axis=1, keepdims=True)
            for h in range(heads)
        ],
        axis=0,
    )


def expand(buf, value, times):
    if times == 1:
        return value
    rows = value.shape[0]
    for half in range(value.shape[1] // 128):
        for j in range(times):
            buf[half, pl.ds(j, rows, stride=times), :] = value[:, half * 128 : half * 128 + 128]
    return jnp.concatenate(
        [buf[half, : rows * times, :] for half in range(value.shape[1] // 128)], axis=1
    )


def pool(buf, value, times):
    if times == 1:
        return value
    rows = value.shape[0] // times
    parts = []
    for half in range(value.shape[1] // 128):
        buf[half, : value.shape[0], :] = value[:, half * 128 : half * 128 + 128]
        total = buf[half, pl.ds(0, rows, stride=times), :]
        for j in range(1, times):
            total = total + buf[half, pl.ds(j, rows, stride=times), :]
        parts.append(total)
    return jnp.concatenate(parts, axis=1)


def kept_left(place, core):
    return lax.rem(place, 2) != core


def near_kernel(place_ref, *refs):
    away_refs, (theirs_ref, go_other_ref, close_ref, close_other_ref) = refs[:6], refs[6:10]
    wh_ref, wl_ref, xh_ref, xl_ref, gh_ref, gl_ref, q_ref, k_ref, v_ref, d_ref = refs[10:20]
    here_refs, sems = refs[20:26], refs[26]
    core = place_ref[1]
    own, width = q_ref.shape
    copies = [
        pltpu.make_async_copy(away, ref, sems.at[j])
        for j, (away, ref) in enumerate(zip(away_refs, here_refs))
    ]
    for copy in copies:
        copy.start()
    here = kept_left(place_ref[0], core)
    for side in range(2):
        kept, other = close_ref[side], close_other_ref[1 - side]
        left = jnp.where(here, kept, other)
        right = jnp.where(here, other, kept)
        xh_ref[side, :own], xl_ref[side, :own] = split(left)
        xh_ref[side, 2 * own :], xl_ref[side, 2 * own :] = split(right)
    middle = slice(own, 2 * own)
    xh_ref[1, middle], xl_ref[1, middle] = split(theirs_ref[...])
    for copy in copies:
        copy.wait()
    tokens_ref, go_ref, *w_refs = here_refs
    xh_ref[0, middle], xl_ref[0, middle] = split(tokens_ref[...])
    gh_ref[0], gl_ref[0] = split(go_ref[...])
    gh_ref[1], gl_ref[1] = split(go_other_ref[...])
    for c in range(2):
        for k, w_ref in enumerate(w_refs[:3]):
            wh_ref[k, c], wl_ref[k, c] = split(w_ref[c * width : (c + 1) * width])
        wh_ref[3, c], wl_ref[3, c] = split(w_refs[3][:, c * width : (c + 1) * width])

    def weight(k, c):
        return wh_ref[k, c], wl_ref[k, c]

    def project(k, start):
        rows = slice(start, start + own)
        return mm((xh_ref[0, rows], xl_ref[0, rows]), weight(k, core), NN) + mm(
            (xh_ref[1, rows], xl_ref[1, rows]), weight(k, 1 - core), NN
        )

    q_ref[...] = project(0, own) * HEAD_DIM ** (-0.5)
    for start in range(0, 3 * own, own):
        k_ref[start : start + own] = project(1, start)
        v_ref[start : start + own] = project(2, start)
    d_ref[...] = mm((gh_ref[0], gl_ref[0]), weight(3, core), NT) + mm(
        (gh_ref[1], gl_ref[1]), weight(3, 1 - core), NT
    )


def near(place, xs, weights):
    own, half = xs[0].shape
    width = weights[0].shape[1]
    vmem = pl.BlockSpec(memory_space=pltpu.VMEM)

    def shape(kind, *s):
        return jax.ShapeDtypeStruct(s, kind)

    return pl.pallas_call(
        near_kernel,
        out_shape=(
            shape(BF16, 4, 2, half, width),
            shape(BF16, 4, 2, half, width),
            shape(BF16, 2, 3 * own, half),
            shape(BF16, 2, 3 * own, half),
            shape(BF16, 2, own, half),
            shape(BF16, 2, own, half),
            shape(F32, own, width),
            shape(F32, 3 * own, width),
            shape(F32, 3 * own, width),
            shape(F32, own, width),
        ),
        in_specs=[pl.BlockSpec(memory_space=pltpu.SMEM)] + [pl.BlockSpec(memory_space=pltpu.HBM)] * 6 + [vmem] * 4,
        out_specs=(vmem,) * 10,
        scratch_shapes=[pltpu.VMEM(x.shape, F32) for x in (*xs[:2], *weights)]
        + [pltpu.SemaphoreType.DMA((6,))],
        compiler_params=pltpu.CompilerParams(vmem_limit_bytes=24 * 2**20),
        cost_estimate=pl.CostEstimate(
            flops=3 * 10**9, bytes_accessed=10 * 2**20, transcendentals=0
        ),
    )(place, *xs[:2], *weights, *xs[2:])


def attend_kernel(
    place_ref, *refs, count, scale,
):
    others_ref, group_ref, group_other_ref = refs[:3]
    pair_refs = refs[3:5]
    wh_ref, wl_ref, xh_ref, xl_ref, gh_ref, gl_ref, q_ref, k_ref, v_ref, d_ref = refs[5:15]
    mine_refs, theirs_refs, dw_ref = refs[15:17], refs[17:19], refs[19]
    k_s, v_s, dk_s, dv_s, xh_s, xl_s, buf = refs[20:]
    own, width = q_ref.shape
    near = 3 * own
    far = 4 * BLOCK
    heads = width // HEAD_DIM
    place = place_ref[0]
    core = place_ref[1]
    line = lax.rem(place, 8)
    edge = jnp.logical_or(place < 4, place >= count - 4)
    over = jnp.logical_or(line < 2, line >= 6)
    sides = ((0, core), (1, 1 - core))

    first = core == 0
    for side, pair_ref in enumerate(pair_refs):
        kept, other = group_ref[side], group_other_ref[1 - side]
        inline, cross = jnp.where(first, kept, other), jnp.where(first, other, kept)
        for j, part in enumerate((others_ref[side], pair_ref[...], inline, cross)):
            rows = slice(j * BLOCK, (j + 1) * BLOCK)
            xh_s[side, rows], xl_s[side, rows] = split(part)

    def weight(k, c):
        return wh_ref[k, c], wl_ref[k, c]

    def far_rows(side, rows=slice(None)):
        return xh_s[side, rows], xl_s[side, rows]

    for start in range(0, far, own):
        rows = slice(start, start + own)
        for k, ref in ((1, k_s), (2, v_s)):
            ref[rows] = sum(mm(far_rows(s, rows), weight(k, c), NN) for s, c in sides)

    jobs = []
    for b in range(own // BLOCK):
        jobs.append((0, b))
    for level in range(1, LEVELS + 1):
        jobs.append((level, 0))
    queries = [q_ref[...]]
    for level in range(1, LEVELS + 1):
        queries.append(pool(buf, q_ref[...], 2**level) * 2.0**-level)

    def keys_of(level, b, ref):
        if level == 0:
            start = own - BLOCK + b * BLOCK
            return ref[0][start : start + 3 * BLOCK]
        if level == 1:
            return jnp.concatenate(
                [0.5 * pool(buf, ref[0][:own], 2), 0.5 * pool(buf, ref[0][2 * own :], 2)]
            )
        start = (level - 2) * 2 * BLOCK
        return ref[1][start : start + 2 * BLOCK]

    def bias_of(level, b):
        keys = 3 * BLOCK if level == 0 else 2 * BLOCK
        col = lax.broadcasted_iota(jnp.int32, (1, keys), 1)
        left, right = place < 1, place >= count - 1
        if level > 1:
            left, right = False, jnp.logical_and(edge, over) if level == 2 else edge
        if level == 0 and b > 0:
            left = False
        if level == 0 and b < own // BLOCK - 1:
            right = False
        bias = jnp.zeros((1, keys), F32)
        if left is not False:
            bias = jnp.where(jnp.logical_and(col < BLOCK, left), MASKED, bias)
        if right is not False:
            bias = jnp.where(jnp.logical_and(col >= keys - BLOCK, right), MASKED, bias)
        return bias

    saved = []
    peaks, dens, nums = [], [], []
    for level, b in jobs:
        rows = BLOCK if level == 0 else queries[level].shape[0]
        query = split(stack_heads(queries[level][b * rows : (b + 1) * rows], heads))
        key = split(keys_of(level, b, (k_ref, k_s)))
        value = split(keys_of(level, b, (v_ref, v_s)))
        scores = mm(query, key, NT) + bias_of(level, b)
        peak = jnp.max(scores, axis=1, keepdims=True)
        weights = jnp.exp(scores - peak)
        den = jnp.sum(weights, axis=1, keepdims=True)
        halves = split(weights)
        num = unstack(mm(halves, value, NN), heads, width)
        saved.append((query, key, value, weights, halves))
        peaks.append(unstack(peak, heads, width))
        dens.append(unstack(den, heads, width))
        nums.append(num)
    blocks = own // BLOCK
    join = lambda parts: [jnp.concatenate(parts[:blocks])] + parts[blocks:]
    peaks, dens, nums = join(peaks), join(dens), join(nums)
    wide_peaks = [expand(buf, p, 2**l) for l, p in enumerate(peaks)]
    top = functools.reduce(jnp.maximum, wide_peaks)
    factors = [2.0**l * jnp.exp(p - top) for l, p in enumerate(wide_peaks)]
    num = sum(f * expand(buf, n, 2**l) for l, (f, n) in enumerate(zip(factors, nums)))
    den = sum(f * expand(buf, n, 2**l) for l, (f, n) in enumerate(zip(factors, dens)))
    inverse = 1.0 / den
    attended = num * inverse
    att = split(attended)

    d_att = d_ref[...]
    for side, c in sides:
        dw_ref[3, c] = mm(att, (gh_ref[side], gl_ref[side]), TN) * scale
    for (target, _), (_, c) in zip((mine_refs, theirs_refs), sides):
        target[near:] = mm(att, weight(3, c), NN)

    r = lax.broadcasted_iota(jnp.int32, (width, width), 0) // HEAD_DIM
    s = lax.broadcasted_iota(jnp.int32, (width, width), 1) // HEAD_DIM
    ones = jnp.where(r == s, 1.0, 0.0).astype(BF16)
    prod = d_att * attended
    p0, p1 = split(prod)
    delta = lax.dot_general(p0, ones, (NN, ((), ())), preferred_element_type=F32)
    delta = delta + lax.dot_general(p1, ones, (NN, ((), ())), preferred_element_type=F32)

    dk_s[...] = jnp.zeros_like(dk_s)
    dv_s[...] = jnp.zeros_like(dv_s)
    d_query = jnp.zeros((own, width), F32)
    level_dq = [[] for _ in range(LEVELS + 1)]
    for (level, b), (query, key, value, weights, halves) in zip(jobs, saved):
        if b == 0:
            share = factors[level] * inverse
            d_num = pool(buf, share * d_att, 2**level)
            d_den = pool(buf, -share * delta, 2**level)
        rows = BLOCK if level == 0 else d_num.shape[0]
        part = slice(b * rows, (b + 1) * rows)
        grad = split(stack_heads(d_num[part], heads))
        d_scores = split(weights * (mm(grad, value, NT) + stack_column(d_den[part], heads)))
        d_value = mm(halves, grad, TN)
        d_key = mm(d_scores, query, TN)
        level_dq[level].append(unstack(mm(d_scores, key, NN), heads, width))
        for ref, grads in ((dk_s, d_key), (dv_s, d_value)):
            if level == 0:
                start = own - BLOCK + b * BLOCK
                ref[start : start + 3 * BLOCK] += grads
            elif level == 1:
                ref[:own] += expand(buf, 0.5 * grads[:BLOCK], 2)
                ref[2 * own : 3 * own] += expand(buf, 0.5 * grads[BLOCK:], 2)
            else:
                start = 3 * own + (level - 2) * 2 * BLOCK
                ref[start : start + 2 * BLOCK] += grads
    for level, parts in enumerate(level_dq):
        d_query = d_query + expand(buf, jnp.concatenate(parts) * 2.0**-level, 2**level)
    dq = split(d_query * HEAD_DIM ** (-0.5))
    dk = split(dk_s[...])
    dv = split(dv_s[...])
    def near_rows(side, rows):
        return xh_ref[side, rows], xl_ref[side, rows]

    every = slice(None)
    for side, c in sides:
        dw_ref[0, c] = mm(near_rows(side, slice(own, 2 * own)), dq, TN) * scale
        for k, grads in ((1, dk), (2, dv)):
            dw_ref[k, c] = scale * (
                mm(near_rows(side, every), cut(grads, slice(near)), TN)
                + mm(far_rows(side), cut(grads, slice(near, near + far)), TN)
            )
    odd = lax.rem(place, 2) == 1
    for (target, far_target), (_, c) in zip((mine_refs, theirs_refs), sides):
        near_dx = []
        for start in range(0, near + far, own):
            rows = slice(start, start + own)
            dx = mm(cut(dk, rows), weight(1, c), NT) + mm(cut(dv, rows), weight(2, c), NT)
            if start == own:
                dx = dx + mm(dq, weight(0, c), NT)
            near_dx.append(dx)
            if start == 2 * own:
                left, _, right = near_dx
                target[:own] = jnp.where(odd, left, right)
                target[rows] = jnp.where(odd, right, left)
            elif start == own:
                target[rows] = dx
            elif start > own:
                far_target[start - near : start - near + own] = dx


def attend(place, xs, known, count, scale):
    half = xs[3].shape[1]
    own, width = known[6].shape
    total = 3 * own + 4 * BLOCK
    rows = 4 * own
    far = 4 * BLOCK
    vmem = pl.BlockSpec(memory_space=pltpu.VMEM)

    def shape(*s):
        return jax.ShapeDtypeStruct(s, F32)

    return pl.pallas_call(
        functools.partial(attend_kernel, count=count, scale=scale),
        out_shape=(
            shape(rows, half),
            shape(far, half),
            shape(rows, half),
            shape(far, half),
            shape(4, 2, half, width),
        ),
        in_specs=[pl.BlockSpec(memory_space=pltpu.SMEM)] + [vmem] * 15,
        out_specs=(vmem,) * 5,
        scratch_shapes=[
            pltpu.VMEM((4 * BLOCK, width), F32),
            pltpu.VMEM((4 * BLOCK, width), F32),
            pltpu.VMEM((total, width), F32),
            pltpu.VMEM((total, width), F32),
            pltpu.VMEM((2, 4 * BLOCK, half), BF16),
            pltpu.VMEM((2, 4 * BLOCK, half), BF16),
            pltpu.VMEM((width // 128, own, 128), F32),
        ],
        compiler_params=pltpu.CompilerParams(vmem_limit_bytes=40 * 2**20),
        cost_estimate=pl.CostEstimate(
            flops=9 * 10**9, bytes_accessed=16 * 2**20, transcendentals=10**6
        ),
    )(place, *xs, *known)


def pool_kernel(own_ref, other_ref, raw_ref, pooled_ref, buf):
    for side, ref in enumerate((own_ref, other_ref)):
        rows = ref[...]
        raw_ref[side] = rows
        pooled_ref[side] = 0.25 * pool(buf, rows, 4)


def pool_tokens(tokens, theirs):
    own, half = tokens.shape
    return pl.pallas_call(
        pool_kernel,
        out_shape=(
            jax.ShapeDtypeStruct((2, own, half), F32),
            jax.ShapeDtypeStruct((2, own // 4, half), F32),
        ),
        scratch_shapes=[pltpu.VMEM((half // 128, own, 128), F32)],
        compiler_params=pltpu.CompilerParams(vmem_limit_bytes=8 * 2**20),
    )(tokens, theirs)


def arrange_kernel(
    place_ref, own_ref, far_ref, far_other_ref, close_ref, close_other_ref,
    pair_ref, others_ref, coarse_ref, buf,
):
    half = BLOCK // 2
    first = place_ref[1] == 0
    for side in range(2):
        far, far_other = far_ref[side], far_other_ref[1 - side]
        two, three = jnp.where(first, far, far_other), jnp.where(first, far_other, far)
        one = jnp.where(first, close_ref[side], close_other_ref[1 - side])
        one = 0.25 * pool(buf, one, 4)
        if side == 0:
            pair_ref[:half] = own_ref[0]
            pair_ref[half:] = one
        others_ref[side, :half] = two
        others_ref[side, half:] = three
        for j, rows in enumerate((own_ref[side], one, two, three)):
            coarse_ref[side, j * half // 2 : (j + 1) * half // 2] = 0.5 * pool(buf, rows, 2)


def arrange(place, pooled, far, far_other, close, close_other):
    own, half = close.shape[1:]
    vmem = pl.BlockSpec(memory_space=pltpu.VMEM)

    def shape(*s):
        return jax.ShapeDtypeStruct(s, F32)

    return pl.pallas_call(
        arrange_kernel,
        out_shape=(shape(BLOCK, half), shape(2, BLOCK, half), shape(2, BLOCK, half)),
        in_specs=[pl.BlockSpec(memory_space=pltpu.SMEM)] + [vmem] * 5,
        out_specs=(vmem,) * 3,
        scratch_shapes=[pltpu.VMEM((half // 128, own, 128), F32)],
        compiler_params=pltpu.CompilerParams(vmem_limit_bytes=8 * 2**20),
    )(place, pooled, far, far_other, close, close_other)


def gather_kernel(own_ref, out_ref, got_ref, pair_ref, inline_ref, total_ref, buf):
    half = BLOCK // 2
    total = own_ref[...] + out_ref[...] + got_ref[half + half // 2 :]
    total = total + expand(buf, 0.25 * (pair_ref[:half] + got_ref[:half]), 4)
    coarse = inline_ref[: half // 2] + got_ref[half : half + half // 2]
    total_ref[...] = total + expand(buf, 0.125 * coarse, 8)


def gather_tokens(own, out, got, pair, inline):
    rows, half = own.shape
    return pl.pallas_call(
        gather_kernel,
        out_shape=jax.ShapeDtypeStruct((rows, half), F32),
        scratch_shapes=[pltpu.VMEM((half // 128, rows, 128), F32)],
        compiler_params=pltpu.CompilerParams(vmem_limit_bytes=8 * 2**20),
    )(own, out, got, pair, inline)


CTX = ("x", "y", "z")
WIDE = ("x", "y")
SWAP = [(0, 1), (1, 0)]


def routes(count):
    beside = [(i, i + 1) for i in range(1, count - 1, 2)]
    mirror = [(i, i - i % 8 + 7 - i % 8) for i in range(count)]
    cross = [(i, i + 15 - 2 * (i % 8)) for i in range(count - 8) if i % 8 >= 4]
    pairs = [(i, 8 * ((i + 2) // 8) + 7 - i % 8) for i in range(count - 2) if i % 8 in (2, 3, 6, 7)]
    return [p + reverse(p) for p in (beside, cross, pairs)] + [mirror]


def reverse(pairs):
    return [(j, i) for i, j in pairs]


def local(tokens, w_query, w_key, w_value, w_out, grad_out):
    count = lax.axis_size(CTX)
    place = lax.axis_index(CTX)
    core = lax.axis_index("head")
    own, half = tokens.shape
    beside, across, pairs, mirror = routes(count)

    def send(rows, pairs):
        return lax.ppermute(rows, CTX, pairs)

    def xor(rows, k):
        return send(rows, [(i, i ^ k) for i in range(count)])

    def swap(rows):
        return lax.ppermute(rows, "head", SWAP)

    def by_core(rows, first, second):
        pairs = [(2 * i + c, 2 * j + c) for c, r in enumerate((first, second)) for i, j in r]
        return lax.ppermute(rows, CTX + ("head",), pairs)

    one, two, three = ([(i, i ^ k) for i in range(count)] for k in (1, 2, 3))
    where = jnp.stack([place, core]).astype(jnp.int32)
    theirs = swap(tokens)
    raw, pooled = pool_tokens(tokens, theirs)
    far, close = by_core(pooled, two, three), by_core(raw, one, beside)
    far, close = lax.optimization_barrier((far, close))
    far_other, close_other = swap(far), swap(close)
    pair, others, coarse = arrange(where, pooled, far, far_other, close, close_other)
    group = by_core(coarse, mirror, across)
    pair = send(pair, pairs)
    close_other, _ = lax.optimization_barrier((close_other, coarse))
    xs = [tokens, grad_out, theirs, swap(grad_out), close, close_other]
    known = near(where, xs, (w_query, w_key, w_value, w_out))
    group, pair, known = lax.optimization_barrier((group, pair, known))
    away = [others, group, swap(group), pair, swap(pair)]
    scale = (own * count) ** (-0.5)
    mine, far_mine, theirs, far_theirs, dw = attend(where, away, known, count, scale)

    wide = lax.axis_size(WIDE)
    others, pair, inline, cross = jnp.split(far_mine + swap(far_theirs), 4)
    one, middle, out, layer_out = jnp.split(mine + swap(theirs), 4)
    part = lax.all_to_all(dw.reshape(wide, -1, half), WIDE, 0, 0)
    pair, inline, cross = send(pair, pairs), send(inline, mirror), send(cross, across)
    part, pair, inline, cross, out = lax.optimization_barrier((part, pair, inline, cross, out))
    out = send(out, beside)
    chunk = part.sum(0)
    for k in (7, 2, 1):
        chunk = chunk + xor(chunk, k)
    chunk, pair, inline, cross, out = lax.optimization_barrier((chunk, pair, inline, cross, out))

    dw = spread(chunk, WIDE, wide).reshape(4, 2 * half, half)
    inline = inline + cross
    got = xor(jnp.concatenate([others, inline[64:]]), 2)
    pair, inline = pair + got[:BLOCK], inline[:64] + got[BLOCK:]
    got = xor(jnp.concatenate([pair[64:], inline[32:], one]), 1)
    grad_tokens = gather_tokens(middle, out, got, pair, inline)
    return (
        layer_out,
        grad_tokens,
        dw[0],
        dw[1],
        dw[2],
        jnp.concatenate([dw[3, :half], dw[3, half:]], axis=1),
    )


def spread(rows, axes, parts):
    return lax.all_to_all(jnp.broadcast_to(rows[None], (parts,) + rows.shape), axes, 0, 0)


def solution(mesh):
    lines = mesh.shape["ctx"] // 8
    split_mesh = jax.sharding.Mesh(
        mesh.devices.reshape(-(-lines // 4), min(lines, 4), 8, 2), ("x", "y", "z", "head")
    )
    placed = (
        P(CTX, "head"),
        P(None, "head"),
        P(None, "head"),
        P(None, "head"),
        P("head", None),
        P(CTX, "head"),
    )
    return jax.shard_map(
        local,
        mesh=split_mesh,
        in_specs=placed,
        out_specs=(P(CTX, "head"),) * 2 + (P(None, "head"),) * 3 + (P("head", None),),
        check_vma=False,
    )
```
